256 devices in a mesh: wave: 128 (over x, y, z), lev: 2 (over core).
Axes of the slice: x: 4, y: 4, z: 8, core: 2. Of those that a mesh axis runs over, the one named last changes fastest.
Arguments:
- spectra: bfloat16 [1280, 192, 1280], P('wave', 'lev'), may hold values from -0.19921875 to 0.19921875
- legendre: bfloat16 [1280, 128, 1280], P('wave'), may hold values from -0.15625 to 0.15625
- wave_slots: int32 [1280], replicated, may hold values from 0 to 1279, as said below
- row_length: int32 [256], P('wave'), may hold values from 20 to 5136, as said below
Outputs:
- grid_out: bfloat16 [256, 96, 5136], P('wave', None, 'lev')
The draws below stay inside these ranges and needn't reach their ends.
Inputs may be any that keep to these rules, and one draw needn't show every extreme that they name: `wave_slots`: a permutation of 0 to 1279 in which slots 2k and 2k+1 hold m and 1279 - m. Each value is 20 plus four times a whole number below 1280; row_length[128 + i] equals row_length[i].
All inputs are finite; a program needn't handle non-finite values.
Results may differ from the reference program's by a relative error of at most 0.0061.
Values may be sent and summed in bfloat16 or wider, within the bound.
No kernel may reach another device: no remote copies, remote signals or barrier semaphores. Data moves between devices by JAX's collectives and lax.ppermute only.
A program may use at most 256 MiB of HBM per device.

```python
import jax
import jax.numpy as jnp
from jax import lax

M = 1280
LATS = 256
HALF = 128
LON = 5136
FL = 96


def draw_wave_slots(key, part):
    key = jax.random.fold_in(key, 3)
    paired = jax.random.permutation(key, M // 2).astype(jnp.int32)
    return jnp.stack([paired, M - 1 - paired], axis=1).reshape(M)


def draw_row_length(key, part):
    key = jax.random.fold_in(key, 5)
    first_key, second_key = jax.random.split(key)
    steps_north = jax.random.randint(first_key, (HALF,), 0, M, dtype=jnp.int32)
    widest = jax.random.randint(second_key, (), 0, HALF, dtype=jnp.int32)
    steps_north = jnp.where(jnp.arange(HALF, dtype=jnp.int32) == widest, M - 1, steps_north)
    lengths = 20 + 4 * steps_north
    return jnp.concatenate([lengths, lengths]).astype(jnp.int32)


def level_of(own_key, shape, shards, least, high):
    level, own = 1.0, jax.random.fold_in(own_key, 6)
    for dim, shards_of in shards:
        draws = jnp.exp(jax.random.uniform(jax.random.fold_in(own, dim), (shards_of,), jnp.float32, least / len(shards), high / len(shards)))
        level = level * jnp.repeat(draws, shape[dim] // shards_of).reshape([-1 if axis == dim else 1 for axis in range(len(shape))])
    return level


def noise(key, shape, width, limit, pieces=(), kind=jnp.bfloat16):
    factor_of = level_of(key, shape, pieces, -0.22, 0.18) if pieces else 1.0
    result = jax.random.normal(key, shape, jnp.float32) * width * factor_of
    return jnp.minimum(jnp.maximum(result, -limit), limit).astype(kind)


def setup_inputs(seed: int = 0) -> dict:
    streams_of = jax.random.split(jax.random.key(seed), 5)
    spectra = noise(streams_of[0], (M, 2 * FL, M), 0.03, 0.19921875, ((0, 128), (1, 2)))
    legendre = noise(streams_of[1], (M, HALF, M), M ** -0.5, 0.15625, ((0, 128),))
    wave_slots = draw_wave_slots(jax.random.fold_in(streams_of[4], 71), 0)
    row_length = draw_row_length(jax.random.fold_in(streams_of[4], 71), 0)
    return {"spectra": spectra, "legendre": legendre, "wave_slots": wave_slots, "row_length": row_length}


def twiddles(wave_list, length, starts):
    phases = (wave_list[:, None] * starts[None, :]) % length
    angles = (2.0 * jnp.pi) * phases.astype(jnp.float32) / length.astype(jnp.float32)
    return jnp.cos(angles), jnp.sin(angles)


def half_row(band_real, band_imag, wave_list, length, side, half_width):
    count = -(-half_width // 512)
    starts = side * half_width + 512 * jnp.arange(count, dtype=jnp.int32)
    cos_a, sin_a = twiddles(wave_list, length, starts)
    cos_b, sin_b = twiddles(wave_list, length, jnp.arange(512, dtype=jnp.int32))
    weights = jnp.where(wave_list == 0, 1.0, 2.0).astype(jnp.float32)
    weights = jnp.where(wave_list <= (length - 1) // 2, weights, 0.0).astype(jnp.float32)
    real_part = band_real.astype(jnp.float32) * weights[:, None]
    imag_part = band_imag.astype(jnp.float32) * weights[:, None]
    turned_real = (real_part[:, None, :] * cos_a[:, :, None] - imag_part[:, None, :] * sin_a[:, :, None]).astype(jnp.bfloat16)
    turned_imag = (real_part[:, None, :] * sin_a[:, :, None] + imag_part[:, None, :] * cos_a[:, :, None]).astype(jnp.bfloat16)
    offset_cos = cos_b.astype(jnp.bfloat16).astype(jnp.float32)
    offset_sin = (-sin_b).astype(jnp.bfloat16).astype(jnp.float32)
    values = jnp.einsum("mak,mb->kab", turned_real.astype(jnp.float32), offset_cos)
    values = values + jnp.einsum("mak,mb->kab", turned_imag.astype(jnp.float32), offset_sin)
    values = values.reshape(values.shape[0], count * 512)[:, :half_width]
    columns = side * half_width + jnp.arange(half_width, dtype=jnp.int32)
    return jnp.where(columns[None, :] < length, values, 0.0)


def reference(spectra, legendre, wave_slots, row_length):
    total_m = spectra.shape[0]
    degrees = spectra.shape[2]
    fields = spectra.shape[1] // 2

    def legendre_slot(inputs):
        north_table, spectrum, wavenumber = inputs
        degree = jnp.arange(degrees, dtype=jnp.int32)
        kept_mask = (degree >= (wavenumber // 64) * 64).astype(jnp.bfloat16)
        parity_signs = (1 - 2 * ((degree - wavenumber) % 2)).astype(jnp.bfloat16)
        full_table = jnp.concatenate([north_table, north_table * parity_signs[None, :]], axis=0)
        kept = spectrum * kept_mask[None, :]
        return jnp.dot(kept, full_table.T, preferred_element_type=jnp.float32).astype(jnp.bfloat16)

    band_values = lax.map(legendre_slot, (legendre, spectra, wave_slots))
    band_values = jnp.transpose(band_values, (0, 2, 1)).reshape(total_m, LATS, fields, 2)
    half_width = LON // 2

    def transform_row(inputs):
        band_rows, length = inputs
        band_real = band_rows[:, :, 0]
        band_imag = band_rows[:, :, 1]
        north_part = half_row(band_real, band_imag, wave_slots, length, 0, half_width)
        south_part = half_row(band_real, band_imag, wave_slots, length, 1, half_width)
        return jnp.concatenate([north_part, south_part], axis=1).astype(jnp.bfloat16)

    return lax.map(transform_row, (jnp.moveaxis(band_values, 1, 0), row_length))
```

```python
import functools
import math

import jax
import jax.numpy as jnp
from jax import lax
from jax.experimental import pallas as pl
from jax.experimental.pallas import tpu as pltpu
from jax.sharding import PartitionSpec as P

BLOCK = 512
NT = (((1,), (1,)), ((), ()))
CHUNK = 256


def legendre_kernel(waves, first, legendre, spectra, sent, tables, spectrum, product, rows, sems):
    slots, columns, degrees = spectrum.shape
    chunks = degrees // CHUNK

    def each(slot, act):
        chunk = waves[first[0] + slot] // CHUNK
        for number in range(chunks):
            kept = pl.ds(number * CHUNK, degrees - number * CHUNK)

            @pl.when(chunk == number)
            def _():
                act(
                    kept,
                    pltpu.make_async_copy(
                        legendre.at[slot, :, kept], tables.at[slot, :, kept], sems.at[slot, 0]
                    ),
                    pltpu.make_async_copy(
                        spectra.at[slot, :, kept], spectrum.at[slot, :, kept], sems.at[slot, 1]
                    ),
                )

    def begin(kept, one, two):
        one.start()
        two.start()

    @pl.loop(0, slots)
    def _(slot):
        each(slot, begin)

    for hemisphere in (0, 1):
        for lat in (0, 1):
            rows[pl.ds(hemisphere * 1024 + lat * 8, 64, stride=16), :] = jnp.zeros(
                (64, 128), jnp.float32
            )
    lane = lax.broadcasted_iota(jnp.int32, (64, 128), 1)
    blank = 128 - columns

    @pl.loop(0, slots)
    def _(slot):
        wave = waves[first[0] + slot]

        def sums(kept, one, two):
            one.wait()
            two.wait()
            degree = lax.broadcasted_iota(jnp.int32, (1, kept.size), 1) + kept.start
            mask = jnp.where(degree >= wave // 64 * 64, 1.0, 0.0)
            signed = jnp.where((degree - wave) % 2 == 0, mask, -mask).astype(jnp.bfloat16)
            mask = mask.astype(jnp.bfloat16)
            own = spectrum[slot, :, kept]
            zero = jnp.zeros((blank, kept.size), jnp.bfloat16)
            both = lax.dot_general(
                tables[slot, :, kept],
                jnp.concatenate([own * mask, zero, own * signed, zero], axis=0),
                NT,
                preferred_element_type=jnp.float32,
            )
            product[0:128] = both[:, 0:128]
            product[128:256] = both[:, 128:256]

        each(slot, sums)
        place = slot * columns // 128
        shift = slot * columns % 128
        for hemisphere in (0, 1):
            for lat in (0, 1):
                band = pltpu.roll(product[pl.ds(hemisphere * 128 + lat, 64, stride=2), :], shift, 1)
                base = hemisphere * 1024 + lat * 8 + place
                here, after = pl.ds(base, 64, stride=16), pl.ds(base + 1, 64, stride=16)
                rows[here, :] = jnp.where(lane >= shift, band, rows[here, :])
                rows[after, :] = jnp.where(lane < shift, band, 0.0)

    sent[...] = rows[...].astype(jnp.bfloat16).reshape(sent.shape)


def legendre_call(waves, first, legendre, spectra):
    slots, lats, degrees = legendre.shape
    columns = spectra.shape[1]
    return pl.pallas_call(
        legendre_kernel,
        out_shape=jax.ShapeDtypeStruct((128, 16, 128), jnp.bfloat16),
        in_specs=[pl.BlockSpec(memory_space=pltpu.SMEM)] * 2 + [pl.BlockSpec(memory_space=pl.ANY)] * 2,
        out_specs=pl.BlockSpec(memory_space=pltpu.VMEM),
        scratch_shapes=[
            pltpu.VMEM((slots, lats, degrees), jnp.bfloat16),
            pltpu.VMEM((slots, columns, degrees), jnp.bfloat16),
            pltpu.VMEM((2 * lats, 128), jnp.float32),
            pltpu.VMEM((2048, 128), jnp.float32),
            pltpu.SemaphoreType.DMA((slots, 2)),
        ],
        compiler_params=pltpu.CompilerParams(vmem_limit_bytes=60 << 20),
        name="legendre",
    )(waves, first, legendre, spectra)


def circle(waves, starts, length):
    whole = waves * starts
    turns = jnp.floor(whole * (1.0 / length))
    phase = whole - turns * length
    phase = jnp.where(phase < 0.0, phase + length, phase)
    phase = jnp.where(phase >= length, phase - length, phase)
    angle = (2.0 * math.pi) * phase / length
    return jnp.cos(angle), jnp.sin(angle)


def table_kernel(half_width, scalars, waves_ref, table, turns, coarse_cos, coarse_sin):
    total = waves_ref.shape[1]
    lat = pl.program_id(0)
    row_length = scalars[lat]
    length = jnp.full((1, total), row_length, jnp.int32).astype(jnp.float32)
    wave = waves_ref[...]
    waves = wave.astype(jnp.float32)
    start = scalars[2] * half_width
    weight = jnp.where(wave == 0, 1.0, 2.0)
    weight = jnp.where(wave <= (row_length - 1) // 2, weight, 0.0)
    eight = lax.broadcasted_iota(jnp.int32, (8, total), 0)
    cos_a, sin_a = circle(waves, (eight * BLOCK + start).astype(jnp.float32), length)
    turns[0, 0:8] = cos_a * weight
    turns[0, 8:16] = sin_a * weight
    coarse = lax.broadcasted_iota(jnp.int32, coarse_cos.shape, 0) * 16
    coarse_cos[...], coarse_sin[...] = circle(waves, coarse.astype(jnp.float32), length)
    fine = lax.broadcasted_iota(jnp.int32, (16, total), 0)
    fine_cos, fine_sin = circle(waves, fine.astype(jnp.float32), length)

    @pl.loop(0, table.shape[1] // 16)
    def _(step):
        cos_u, sin_u = coarse_cos[pl.ds(step, 1), :], coarse_sin[pl.ds(step, 1), :]
        at = pl.ds(pl.multiple_of(step * 16, 16), 16)
        table[0, at, 0:total] = (cos_u * fine_cos - sin_u * fine_sin).astype(jnp.bfloat16)
        table[0, at, total:] = (-(sin_u * fine_cos + cos_u * fine_sin)).astype(jnp.bfloat16)


def table_call(scalars, waves, half_width):
    total = waves.shape[1]
    rows = BLOCK + 16
    return pl.pallas_call(
        functools.partial(table_kernel, half_width),
        out_shape=[
            jax.ShapeDtypeStruct((2, rows, 2 * total), jnp.bfloat16),
            jax.ShapeDtypeStruct((2, 16, total), jnp.float32),
        ],
        grid_spec=pltpu.PrefetchScalarGridSpec(
            num_scalar_prefetch=1,
            grid=(2,),
            in_specs=[pl.BlockSpec((1, total), lambda l, s: (0, 0))],
            out_specs=[
                pl.BlockSpec((1, rows, 2 * total), lambda l, s: (l, 0, 0)),
                pl.BlockSpec((1, 16, total), lambda l, s: (l, 0, 0)),
            ],
            scratch_shapes=[pltpu.VMEM((40, total), jnp.float32)] * 2,
        ),
        compiler_params=pltpu.CompilerParams(vmem_limit_bytes=32 << 20),
        cost_estimate=pl.CostEstimate(
            flops=20_000_000, bytes_accessed=6_000_000, transcendentals=400_000
        ),
        name="tables",
    )(scalars, waves)


def fourier_kernel(half_width, fields, count, scalars, *refs):
    arrivals = refs[:count]
    table_ref, turns, out, table, rows, bands, turned, sems = refs[count:]
    total = turns.shape[2]
    lat = pl.program_id(0)
    row_length = scalars[lat]
    lev = scalars[2]
    start = lev * half_width
    pieces = half_width // BLOCK
    copies = [
        pltpu.make_async_copy(table_ref.at[number], table.at[number], sems.at[number])
        for number in (0, 1)
    ]

    @pl.when(lat == 0)
    def _():
        for copy in copies:
            copy.start()
        for number, arrived in enumerate(arrivals):
            rows[number] = arrived[...].astype(jnp.float32).reshape(2048, 128)

    i = lax.broadcasted_iota(jnp.int32, (128, 128), 0)
    j = lax.broadcasted_iota(jnp.int32, (128, 128), 1)
    source = i // 32 * 32 + jnp.where(i % 32 < 16, 2 * (i % 16), 2 * (i % 16) + 1)
    sort = jnp.where(source == j, 1.0, 0.0).astype(jnp.bfloat16)
    for number in range(count):
        for place in range(8):
            part = rows[number, pl.ds(lat * 8 + place, 128, stride=16), :].astype(jnp.bfloat16)
            bands[place * 128 : place * 128 + 128] = lax.dot_general(
                sort, part, NT, preferred_element_type=jnp.float32
            )

        @pl.loop(0, total // 128)
        def _(slot):
            at = pl.ds(pl.multiple_of(slot * 128, 128), 128)
            behind = pl.ds(pl.multiple_of(total + slot * 128, 128), 128)
            base = slot * (2 * fields)
            for third in range(fields // 16):
                real = bands[pl.ds(pl.multiple_of(base + third * 32, 16), 16), :]
                imag = bands[pl.ds(pl.multiple_of(base + third * 32 + 16, 16), 16), :]
                for piece in range(pieces):
                    cos_a = turns[lat, piece : piece + 1, at]
                    sin_a = turns[lat, 8 + piece : 9 + piece, at]
                    row = (number * pieces + piece) * fields + third * 16
                    turned[row : row + 16, at] = (real * cos_a - imag * sin_a).astype(jnp.bfloat16)
                    turned[row : row + 16, behind] = (real * sin_a + imag * cos_a).astype(
                        jnp.bfloat16
                    )

    for number in (0, 1):

        @pl.when(lat == number)
        def _():
            copies[number].wait()

    values = lax.dot_general(
        turned[...], table[lat, 0:BLOCK], NT, preferred_element_type=jnp.float32
    )
    column = lax.broadcasted_iota(jnp.int32, (1, BLOCK), 1) + start
    for number in range(count):
        level = pl.ds(pl.multiple_of((lev if number == 0 else 1 - lev) * fields, 16), fields)
        for piece in range(pieces):
            base = (number * pieces + piece) * fields
            kept = column + piece * BLOCK < row_length
            out[0, level, piece * BLOCK : piece * BLOCK + BLOCK] = jnp.where(
                kept, values[base : base + fields], 0.0
            ).astype(jnp.bfloat16)
        tail = lax.dot_general(
            turned[base : base + fields],
            table[lat, BLOCK : BLOCK + 16],
            NT,
            preferred_element_type=jnp.float32,
        )
        kept = lax.broadcasted_iota(jnp.int32, (1, 16), 1) + (start + pieces * BLOCK) < row_length
        out[0, level, pieces * BLOCK :] = jnp.where(kept, tail, 0.0)[:, 0:8].astype(jnp.bfloat16)


def fourier_call(scalars, arrivals, table, turns, half_width, fields):
    count = len(arrivals)
    pieces = half_width // BLOCK
    return pl.pallas_call(
        functools.partial(fourier_kernel, half_width, fields, count),
        out_shape=jax.ShapeDtypeStruct((2, 2 * fields, half_width), jnp.bfloat16),
        grid_spec=pltpu.PrefetchScalarGridSpec(
            num_scalar_prefetch=1,
            grid=(2,),
            in_specs=[pl.BlockSpec(memory_space=pltpu.VMEM)] * count
            + [pl.BlockSpec(memory_space=pl.ANY), pl.BlockSpec(memory_space=pltpu.VMEM)],
            out_specs=pl.BlockSpec((1, 2 * fields, half_width), lambda l, s: (l, 0, 0)),
            scratch_shapes=[
                pltpu.VMEM(table.shape, jnp.bfloat16),
                pltpu.VMEM((count, 2048, 128), jnp.float32),
                pltpu.VMEM((1024, 128), jnp.float32),
                pltpu.VMEM((count * pieces * fields, table.shape[2]), jnp.bfloat16),
                pltpu.SemaphoreType.DMA((2,)),
            ],
        ),
        compiler_params=pltpu.CompilerParams(vmem_limit_bytes=58 << 20),
        name="fourier",
    )(scalars, *arrivals, table, turns)


def on_device(spectra, legendre, wave_slots, row_length):
    slots = spectra.shape[0]
    fields = spectra.shape[1] // 2
    total = wave_slots.shape[0]
    half_width = (4 * total + 16) // 2
    first = (lax.axis_index("wave") * slots).astype(jnp.int32)[None]
    lev = lax.axis_index("lev").astype(jnp.int32)
    scalars = jnp.concatenate([row_length, lev[None]])
    waves = wave_slots.reshape(total // slots, slots).T.reshape(1, total)
    sent = legendre_call(wave_slots, first, legendre, spectra)
    arrived = lax.all_to_all(sent, "wave", split_axis=0, concat_axis=0, tiled=True)
    table, turns = table_call(scalars, waves, half_width)
    arrived, table, turns = lax.optimization_barrier((arrived, table, turns))
    other = lax.ppermute(arrived, "lev", [(0, 1), (1, 0)])
    return fourier_call(scalars, (arrived, other), table, turns, half_width, fields)


def solution(mesh):
    placed = (P("wave", "lev", None), P("wave", None, None), P(), P("wave"))
    return jax.shard_map(
        on_device, mesh=mesh, in_specs=placed, out_specs=P("wave", None, "lev"), check_vma=False
    )
```

```python
import functools
import math

import jax
import jax.numpy as jnp
from jax import lax
from jax.experimental import pallas as pl
from jax.experimental.pallas import tpu as pltpu
from jax.sharding import PartitionSpec as P

BLOCK = 512
NT = (((1,), (1,)), ((), ()))
CHUNK = 256


def legendre_kernel(waves_ref, legendre, spectra, sent, waves, tables, spectrum, sums, rows, sems, wave_sem):
    slots, columns, degrees = spectrum.shape
    lats = tables.shape[1]
    steps = degrees // CHUNK + 1
    copies = [
        (
            pltpu.make_async_copy(legendre.at[slot], tables.at[slot], sems.at[slot, 0]),
            pltpu.make_async_copy(spectra.at[slot], spectrum.at[slot], sems.at[slot, 1]),
        )
        for slot in range(slots)
    ]
    fetch = pltpu.make_async_copy(waves_ref, waves, wave_sem)
    fetch.start()
    for both in copies:
        for copy in both:
            copy.start()
    first = lax.axis_index("wave") * slots
    sums[...] = jnp.zeros_like(sums)
    i = lax.broadcasted_iota(jnp.int32, (lats, lats), 0)
    j = lax.broadcasted_iota(jnp.int32, (lats, lats), 1)
    same = jnp.where(i == j, 1.0, 0.0).astype(jnp.bfloat16)
    fetch.wait()
    for pair in range(slots // 2):
        for slot in (2 * pair, 2 * pair + 1):
            for copy in copies[slot]:
                copy.wait()
        wave = waves[first + 2 * pair]
        skipped = wave // CHUNK
        split = steps - 1 - skipped
        for step in range(steps):
            later = step >= split
            slot = 2 * pair + later.astype(jnp.int32)
            start = pl.multiple_of(jnp.where(later, step - 1, skipped + step) * CHUNK, CHUNK)
            number = jnp.where(later, degrees - 1 - wave, wave)
            degree = lax.broadcasted_iota(jnp.int32, (1, CHUNK), 1) + start
            mask = jnp.where(degree >= number // 64 * 64, 1.0, 0.0)
            signed = jnp.where((degree - number) % 2 == 0, mask, -mask).astype(jnp.bfloat16)
            own = spectrum[slot, :, pl.ds(start, CHUNK)]
            both = lax.dot_general(
                jnp.concatenate([own * mask.astype(jnp.bfloat16), own * signed], axis=0),
                tables[slot, :, pl.ds(start, CHUNK)],
                NT,
                preferred_element_type=jnp.float32,
            )
            at = pl.ds(pl.multiple_of(slot * columns, 32), columns)
            sums[0, at, :] += both[0:columns]
            sums[1, at, :] += both[columns:]
        done = [pair * 2 * columns // 128, (pair + 1) * 2 * columns // 128]
        for part in range(done[0], done[1] if pair < slots // 2 - 1 else 8):
            for side in (0, 1):
                rows[pl.ds(side * 1024 + part, lats, stride=8), :] = lax.dot_general(
                    same,
                    sums[side, part * 128 : part * 128 + 128].astype(jnp.bfloat16),
                    NT,
                    preferred_element_type=jnp.float32,
                )
    sent[...] = rows[...].astype(jnp.bfloat16).reshape(sent.shape)


def legendre_call(waves, legendre, spectra):
    slots, lats, degrees = legendre.shape
    columns = spectra.shape[1]
    return pl.pallas_call(
        legendre_kernel,
        out_shape=jax.ShapeDtypeStruct((128, 16, 128), jnp.bfloat16),
        in_specs=[pl.BlockSpec(memory_space=pl.ANY)] * 3,
        out_specs=pl.BlockSpec(memory_space=pltpu.VMEM),
        scratch_shapes=[
            pltpu.SMEM(waves.shape, jnp.int32),
            pltpu.VMEM((slots, lats, degrees), jnp.bfloat16),
            pltpu.VMEM((slots, columns, degrees), jnp.bfloat16),
            pltpu.VMEM((2, 1024, lats), jnp.float32),
            pltpu.VMEM((2048, 128), jnp.float32),
            pltpu.SemaphoreType.DMA((slots, 2)),
            pltpu.SemaphoreType.DMA,
        ],
        compiler_params=pltpu.CompilerParams(vmem_limit_bytes=60 << 20),
        name="legendre",
    )(waves, legendre, spectra)


def circle(waves, starts, length):
    whole = waves * starts
    turns = jnp.floor(whole * (1.0 / length))
    phase = whole - turns * length
    phase = jnp.where(phase < 0.0, phase + length, phase)
    phase = jnp.where(phase >= length, phase - length, phase)
    angle = (2.0 * math.pi) * phase / length
    return jnp.cos(angle), jnp.sin(angle)


def table_kernel(half_width, scalars, waves_ref, table, turns, coarse_cos, coarse_sin):
    total = waves_ref.shape[1]
    lat = pl.program_id(0)
    row_length = scalars[lat]
    length = jnp.full((1, total), row_length, jnp.int32).astype(jnp.float32)
    wave = waves_ref[...]
    waves = wave.astype(jnp.float32)
    start = scalars[2] * half_width
    weight = jnp.where(wave == 0, 1.0, 2.0)
    weight = jnp.where(wave <= (row_length - 1) // 2, weight, 0.0)
    eight = lax.broadcasted_iota(jnp.int32, (8, total), 0)
    cos_a, sin_a = circle(waves, (eight * BLOCK + start).astype(jnp.float32), length)
    turns[0, 0:8] = cos_a * weight
    turns[0, 8:16] = sin_a * weight
    coarse = lax.broadcasted_iota(jnp.int32, coarse_cos.shape, 0) * 16
    coarse_cos[...], coarse_sin[...] = circle(waves, coarse.astype(jnp.float32), length)
    fine = lax.broadcasted_iota(jnp.int32, (16, total), 0)
    fine_cos, fine_sin = circle(waves, fine.astype(jnp.float32), length)

    @pl.loop(0, table.shape[1] // 16)
    def _(step):
        cos_u, sin_u = coarse_cos[pl.ds(step, 1), :], coarse_sin[pl.ds(step, 1), :]
        at = pl.ds(pl.multiple_of(step * 16, 16), 16)
        table[0, at, 0:total] = (cos_u * fine_cos - sin_u * fine_sin).astype(jnp.bfloat16)
        table[0, at, total:] = (-(sin_u * fine_cos + cos_u * fine_sin)).astype(jnp.bfloat16)


def table_call(scalars, waves, half_width):
    total = waves.shape[1]
    rows = BLOCK + 16
    return pl.pallas_call(
        functools.partial(table_kernel, half_width),
        out_shape=[
            jax.ShapeDtypeStruct((2, rows, 2 * total), jnp.bfloat16),
            jax.ShapeDtypeStruct((2, 16, total), jnp.float32),
        ],
        grid_spec=pltpu.PrefetchScalarGridSpec(
            num_scalar_prefetch=1,
            grid=(2,),
            in_specs=[pl.BlockSpec((1, total), lambda l, s: (0, 0))],
            out_specs=[
                pl.BlockSpec((1, rows, 2 * total), lambda l, s: (l, 0, 0)),
                pl.BlockSpec((1, 16, total), lambda l, s: (l, 0, 0)),
            ],
            scratch_shapes=[pltpu.VMEM((40, total), jnp.float32)] * 2,
        ),
        compiler_params=pltpu.CompilerParams(vmem_limit_bytes=32 << 20),
        cost_estimate=pl.CostEstimate(
            flops=20_000_000, bytes_accessed=6_000_000, transcendentals=400_000
        ),
        name="tables",
    )(scalars, waves)


def fourier_kernel(
    fields,
    lengths_ref,
    own,
    other,
    table_ref,
    turns_ref,
    out_ref,
    lengths,
    arrived,
    table,
    turns,
    rows,
    parts,
    bands,
    first,
    second,
    out,
    sems,
):
    half_width = out.shape[2]
    total = turns.shape[2]
    pieces = half_width // BLOCK
    thirds = fields // 16
    half = BLOCK // 2
    lev = lax.axis_index("lev")
    start = lev * half_width
    fetch = [
        pltpu.make_async_copy(own, arrived.at[0], sems.at[0]),
        pltpu.make_async_copy(other, arrived.at[1], sems.at[1]),
        pltpu.make_async_copy(turns_ref, turns, sems.at[2]),
        pltpu.make_async_copy(lengths_ref, lengths, sems.at[3]),
    ]
    tables = [
        pltpu.make_async_copy(table_ref.at[lat], table.at[lat], sems.at[4 + lat]) for lat in (0, 1)
    ]
    results = [
        pltpu.make_async_copy(out.at[lat], out_ref.at[lat], sems.at[6 + lat]) for lat in (0, 1)
    ]
    for copy in fetch:
        copy.start()
    tables[0].start()
    i = lax.broadcasted_iota(jnp.int32, (128, 128), 0)
    j = lax.broadcasted_iota(jnp.int32, (128, 128), 1)
    source = i // 32 * 32 + jnp.where(i % 32 < 16, 2 * (i % 16), 2 * (i % 16) + 1)
    sort = jnp.where(source == j, 1.0, 0.0).astype(jnp.bfloat16)
    for number in (0, 1):
        fetch[number].wait()
        if number == 1:
            tables[1].start()
        rows[number] = arrived[number].astype(jnp.float32).reshape(2048, 128)
        for lat in (0, 1):
            for place in range(8):
                parts[lat, number, place * 128 : place * 128 + 128] = rows[
                    number, pl.ds(lat * 8 + place, 128, stride=16), :
                ].astype(jnp.bfloat16)
            bands[lat, number] = lax.dot_general(
                sort, parts[lat, number], NT, preferred_element_type=jnp.float32
            )

    def turn(lat, slot, turned):
        at = pl.ds(pl.multiple_of(slot * 128, 128), 128)
        behind = pl.ds(pl.multiple_of(total + slot * 128, 128), 128)
        for third in range(thirds):
            group = slot * thirds + third
            lanes = pl.ds(pl.multiple_of(group // 4 * 128, 128), 128)
            base = pl.multiple_of(group % 4 * 32, 32)
            for number in (0, 1):
                real = bands[lat, number, pl.ds(base, 16), lanes]
                imag = bands[lat, number, pl.ds(base + 16, 16), lanes]
                for piece in range(pieces):
                    cos_a = turns[lat, piece : piece + 1, at]
                    sin_a = turns[lat, 8 + piece : 9 + piece, at]
                    row = (piece * 2 + number) * fields + third * 16
                    turned[row : row + 16, at] = (real * cos_a - imag * sin_a).astype(jnp.bfloat16)
                    turned[row : row + 16, behind] = (real * sin_a + imag * cos_a).astype(
                        jnp.bfloat16
                    )

    def levels(number):
        return pl.ds(pl.multiple_of((lev if number == 0 else 1 - lev) * fields, 16), fields)

    def multiply(lat, side, turned):
        behind = pl.multiple_of(side * half, half)
        values = lax.dot_general(
            turned[...], table[lat, pl.ds(behind, half), :], NT, preferred_element_type=jnp.float32
        )
        column = lax.broadcasted_iota(jnp.int32, (1, half), 1) + (start + behind)
        for piece in range(pieces):
            kept = column + piece * BLOCK < lengths[lat]
            for number in (0, 1):
                row = (piece * 2 + number) * fields
                out[lat, levels(number), pl.ds(piece * BLOCK + behind, half)] = jnp.where(
                    kept, values[row : row + fields], 0.0
                ).astype(jnp.bfloat16)

    def finish(lat, turned):
        tail = lax.dot_general(
            turned[(pieces - 1) * 2 * fields :],
            table[lat, BLOCK : BLOCK + 16],
            NT,
            preferred_element_type=jnp.float32,
        )
        column = lax.broadcasted_iota(jnp.int32, (1, 16), 1) + (start + pieces * BLOCK)
        tail = jnp.where(column < lengths[lat], tail, 0.0)[:, 0 : half_width - pieces * BLOCK]
        for number in (0, 1):
            out[lat, levels(number), pieces * BLOCK :] = tail[
                number * fields : number * fields + fields
            ].astype(jnp.bfloat16)
        results[lat].start()

    fetch[2].wait()
    fetch[3].wait()

    @pl.loop(0, total // 128)
    def _(slot):
        turn(0, slot, first)

    tables[0].wait()
    count = total // 128 // 2

    @pl.loop(0, 2)
    def _(side):
        for step in range(count):
            turn(1, side * count + step, second)
        multiply(0, side, first)

    finish(0, first)
    tables[1].wait()

    @pl.loop(0, 2)
    def _(side):
        multiply(1, side, second)

    finish(1, second)
    results[0].wait()
    results[1].wait()


def fourier_call(lengths, own, other, table, turns, half_width, fields):
    pieces = half_width // BLOCK
    turned = pltpu.VMEM((2 * pieces * fields, table.shape[2]), jnp.bfloat16)
    shape = (2, 2 * fields, half_width)
    return pl.pallas_call(
        functools.partial(fourier_kernel, fields),
        out_shape=jax.ShapeDtypeStruct(shape, jnp.bfloat16),
        in_specs=[pl.BlockSpec(memory_space=pl.ANY)] * 5,
        out_specs=pl.BlockSpec(memory_space=pl.ANY),
        scratch_shapes=[
            pltpu.SMEM((2,), jnp.int32),
            pltpu.VMEM((2,) + own.shape, jnp.bfloat16),
            pltpu.VMEM(table.shape, jnp.bfloat16),
            pltpu.VMEM(turns.shape, jnp.float32),
            pltpu.VMEM((2, 2048, 128), jnp.float32),
            pltpu.VMEM((2, 2, 1024, 128), jnp.bfloat16),
            pltpu.VMEM((2, 2, 128, 1024), jnp.float32),
            turned,
            turned,
            pltpu.VMEM(shape, jnp.bfloat16),
            pltpu.SemaphoreType.DMA((8,)),
        ],
        compiler_params=pltpu.CompilerParams(vmem_limit_bytes=58 << 20),
        name="fourier",
    )(lengths, own, other, table, turns)


def on_device(spectra, legendre, wave_slots, row_length):
    slots = spectra.shape[0]
    fields = spectra.shape[1] // 2
    total = wave_slots.shape[0]
    half_width = (4 * total + 16) // 2
    lev = lax.axis_index("lev").astype(jnp.int32)
    scalars = jnp.concatenate([row_length, lev[None]])
    waves = wave_slots.reshape(total // slots, slots).T.reshape(1, total)
    sent = legendre_call(wave_slots, legendre, spectra)
    arrived = lax.all_to_all(sent, "wave", split_axis=0, concat_axis=0, tiled=True)
    table, turns = table_call(scalars, waves, half_width)
    arrived, table, turns = lax.optimization_barrier((arrived, table, turns))
    other = lax.ppermute(arrived, "lev", [(0, 1), (1, 0)])
    return fourier_call(row_length, arrived, other, table, turns, half_width, fields)


def solution(mesh):
    placed = (P("wave", "lev", None), P("wave", None, None), P(), P("wave"))
    return jax.shard_map(
        on_device, mesh=mesh, in_specs=placed, out_specs=P("wave", None, "lev"), check_vma=False
    )
```

```python
import functools
import math

import jax
import jax.numpy as jnp
from jax import lax
from jax.experimental import pallas as pl
from jax.experimental.pallas import tpu as pltpu
from jax.sharding import PartitionSpec as P

BLOCK = 512
PIECES = 5
VMEM = 48 << 20
NT = (((1,), (1,)), ((), ()))
CHUNK = 256


def legendre_kernel(waves_ref, legendre, spectra, sent, waves, tables, spectrum, sums, rows, sems, wave_sem):
    slots, columns, degrees = spectrum.shape
    lats = tables.shape[1]
    steps = degrees // CHUNK + 1
    copies = [
        (
            pltpu.make_async_copy(legendre.at[slot], tables.at[slot], sems.at[slot, 0]),
            pltpu.make_async_copy(spectra.at[slot], spectrum.at[slot], sems.at[slot, 1]),
        )
        for slot in range(slots)
    ]
    fetch = pltpu.make_async_copy(waves_ref, waves, wave_sem)
    fetch.start()
    for both in copies:
        for copy in both:
            copy.start()
    first = lax.axis_index("wave") * slots
    sums[...] = jnp.zeros_like(sums)
    i = lax.broadcasted_iota(jnp.int32, (lats, lats), 0)
    j = lax.broadcasted_iota(jnp.int32, (lats, lats), 1)
    same = jnp.where(i == j, 1.0, 0.0).astype(jnp.bfloat16)
    fetch.wait()
    for pair in range(slots // 2):
        for slot in (2 * pair, 2 * pair + 1):
            for copy in copies[slot]:
                copy.wait()
        wave = waves[first + 2 * pair]
        skipped = wave // CHUNK
        split = steps - 1 - skipped
        for step in range(steps):
            later = step >= split
            slot = 2 * pair + later.astype(jnp.int32)
            start = pl.multiple_of(jnp.where(later, step - 1, skipped + step) * CHUNK, CHUNK)
            number = jnp.where(later, degrees - 1 - wave, wave)
            degree = lax.broadcasted_iota(jnp.int32, (1, CHUNK), 1) + start
            mask = jnp.where(degree >= number // 64 * 64, 1.0, 0.0)
            signed = jnp.where((degree - number) % 2 == 0, mask, -mask).astype(jnp.bfloat16)
            own = spectrum[slot, :, pl.ds(start, CHUNK)]
            both = lax.dot_general(
                jnp.concatenate([own * mask.astype(jnp.bfloat16), own * signed], axis=0),
                tables[slot, :, pl.ds(start, CHUNK)],
                NT,
                preferred_element_type=jnp.float32,
            )
            at = pl.ds(pl.multiple_of(slot * columns, 32), columns)
            sums[0, at, :] += both[0:columns]
            sums[1, at, :] += both[columns:]
        done = [pair * 2 * columns // 128, (pair + 1) * 2 * columns // 128]
        for part in range(done[0], done[1] if pair < slots // 2 - 1 else 8):
            for side in (0, 1):
                rows[pl.ds(side * 1024 + part, lats, stride=8), :] = lax.dot_general(
                    same,
                    sums[side, part * 128 : part * 128 + 128].astype(jnp.bfloat16),
                    NT,
                    preferred_element_type=jnp.float32,
                )
    sent[...] = rows[...].astype(jnp.bfloat16).reshape(sent.shape)


def legendre_call(waves, legendre, spectra):
    slots, lats, degrees = legendre.shape
    columns = spectra.shape[1]
    return pl.pallas_call(
        legendre_kernel,
        out_shape=jax.ShapeDtypeStruct((128, 16, 128), jnp.bfloat16),
        in_specs=[pl.BlockSpec(memory_space=pl.ANY)] * 3,
        out_specs=pl.BlockSpec(memory_space=pltpu.VMEM),
        scratch_shapes=[
            pltpu.SMEM(waves.shape, jnp.int32),
            pltpu.VMEM((slots, lats, degrees), jnp.bfloat16),
            pltpu.VMEM((slots, columns, degrees), jnp.bfloat16),
            pltpu.VMEM((2, 1024, lats), jnp.float32),
            pltpu.VMEM((2048, 128), jnp.float32),
            pltpu.SemaphoreType.DMA((slots, 2)),
            pltpu.SemaphoreType.DMA,
        ],
        compiler_params=pltpu.CompilerParams(vmem_limit_bytes=60 << 20),
        name="legendre",
    )(waves, legendre, spectra)


def circle(waves, starts, length):
    whole = waves * starts
    turns = jnp.floor(whole * (1.0 / length))
    phase = whole - turns * length
    phase = jnp.where(phase < 0.0, phase + length, phase)
    phase = jnp.where(phase >= length, phase - length, phase)
    angle = (2.0 * math.pi) * phase / length
    return jnp.cos(angle), jnp.sin(angle)


def table_kernel(half_width, scalars, waves_ref, table, turns, coarse_cos, coarse_sin):
    total = waves_ref.shape[1]
    lat = pl.program_id(0)
    row_length = scalars[lat]
    length = jnp.full((1, total), row_length, jnp.int32).astype(jnp.float32)
    wave = waves_ref[...]
    waves = wave.astype(jnp.float32)
    start = scalars[2] * half_width
    weight = jnp.where(wave == 0, 1.0, 2.0)
    weight = jnp.where(wave <= (row_length - 1) // 2, weight, 0.0)
    eight = lax.broadcasted_iota(jnp.int32, (8, total), 0)
    cos_a, sin_a = circle(waves, (eight * BLOCK + start).astype(jnp.float32), length)
    turns[0, 0:8] = cos_a * weight
    turns[0, 8:16] = sin_a * weight
    coarse = lax.broadcasted_iota(jnp.int32, coarse_cos.shape, 0) * 16
    coarse_cos[...], coarse_sin[...] = circle(waves, coarse.astype(jnp.float32), length)
    fine = lax.broadcasted_iota(jnp.int32, (16, total), 0)
    fine_cos, fine_sin = circle(waves, fine.astype(jnp.float32), length)

    @pl.loop(0, table.shape[1] // 16)
    def _(step):
        cos_u, sin_u = coarse_cos[pl.ds(step, 1), :], coarse_sin[pl.ds(step, 1), :]
        at = pl.ds(pl.multiple_of(step * 16, 16), 16)
        table[0, at, 0:total] = (cos_u * fine_cos - sin_u * fine_sin).astype(jnp.bfloat16)
        table[0, at, total:] = (-(sin_u * fine_cos + cos_u * fine_sin)).astype(jnp.bfloat16)


def table_call(scalars, waves, half_width):
    total = waves.shape[1]
    rows = BLOCK + 16
    return pl.pallas_call(
        functools.partial(table_kernel, half_width),
        out_shape=[
            jax.ShapeDtypeStruct((2, rows, 2 * total), jnp.bfloat16),
            jax.ShapeDtypeStruct((2, 16, total), jnp.float32),
        ],
        grid_spec=pltpu.PrefetchScalarGridSpec(
            num_scalar_prefetch=1,
            grid=(2,),
            in_specs=[pl.BlockSpec((1, total), lambda l, s: (0, 0))],
            out_specs=[
                pl.BlockSpec((1, rows, 2 * total), lambda l, s: (l, 0, 0)),
                pl.BlockSpec((1, 16, total), lambda l, s: (l, 0, 0)),
            ],
            scratch_shapes=[pltpu.VMEM((40, total), jnp.float32)] * 2,
        ),
        compiler_params=pltpu.CompilerParams(vmem_limit_bytes=32 << 20),
        cost_estimate=pl.CostEstimate(
            flops=20_000_000, bytes_accessed=6_000_000, transcendentals=400_000
        ),
        name="tables",
    )(scalars, waves)


def unpack(arrived, rows, parts, keep):
    rows[...] = arrived[...].astype(jnp.float32).reshape(2048, 128)
    i = lax.broadcasted_iota(jnp.int32, (128, 128), 0)
    j = lax.broadcasted_iota(jnp.int32, (128, 128), 1)
    source = i // 32 * 32 + jnp.where(i % 32 < 16, 2 * (i % 16), 2 * (i % 16) + 1)
    sort = jnp.where(source == j, 1.0, 0.0).astype(jnp.bfloat16)
    for lat in (0, 1):
        for place in range(8):
            parts[lat, place * 128 : place * 128 + 128] = rows[
                pl.ds(lat * 8 + place, 128, stride=16), :
            ].astype(jnp.bfloat16)
        keep[lat][...] = lax.dot_general(sort, parts[lat], NT, preferred_element_type=jnp.float32)


def turn(bands, turns, lat, slot, turned):
    total = turns.shape[2]
    fields = turned.shape[0] // PIECES
    at = pl.ds(pl.multiple_of(slot * 128, 128), 128)
    behind = pl.ds(pl.multiple_of(total + slot * 128, 128), 128)
    for third in range(fields // 16):
        group = slot * (fields // 16) + third
        lanes = pl.ds(pl.multiple_of(group // 4 * 128, 128), 128)
        base = pl.multiple_of(group % 4 * 32, 32)
        real = bands[pl.ds(base, 16), lanes]
        imag = bands[pl.ds(base + 16, 16), lanes]
        for piece in range(PIECES):
            cos_a = turns[lat, piece : piece + 1, at]
            sin_a = turns[lat, 8 + piece : 9 + piece, at]
            row = piece * fields + third * 16
            turned[row : row + 16, at] = (real * cos_a - imag * sin_a).astype(jnp.bfloat16)
            turned[row : row + 16, behind] = (real * sin_a + imag * cos_a).astype(jnp.bfloat16)


def own_kernel(
    lengths, own, table_ref, turns_ref, turned, table, turns, limits, rows, parts, bands, sems
):
    fetch = [
        pltpu.make_async_copy(turns_ref, turns, sems.at[0]),
        pltpu.make_async_copy(table_ref.at[0], table, sems.at[1]),
    ]
    for copy in fetch:
        copy.start()
    for lat in (0, 1):
        limits[8 * lat : 8 * lat + 8] = jnp.full((8, BLOCK), lengths[lat], jnp.int32)
    unpack(own, rows, parts, (bands.at[0], bands.at[1]))
    fetch[0].wait()

    @pl.loop(0, turns.shape[2] // 128)
    def _(slot):
        for lat in (0, 1):
            turn(bands.at[lat], turns, lat, slot, turned.at[lat])

    fetch[1].wait()


def own_call(lengths, own, table, turns, fields):
    return pl.pallas_call(
        own_kernel,
        out_shape=[
            jax.ShapeDtypeStruct((2, PIECES * fields, table.shape[2]), jnp.bfloat16),
            jax.ShapeDtypeStruct(table.shape[1:], jnp.bfloat16),
            jax.ShapeDtypeStruct(turns.shape, jnp.float32),
            jax.ShapeDtypeStruct((16, BLOCK), jnp.int32),
        ],
        in_specs=[
            pl.BlockSpec(memory_space=pltpu.SMEM),
            pl.BlockSpec(memory_space=pltpu.VMEM),
            pl.BlockSpec(memory_space=pl.ANY),
            pl.BlockSpec(memory_space=pl.ANY),
        ],
        out_specs=[pl.BlockSpec(memory_space=pltpu.VMEM)] * 4,
        scratch_shapes=[
            pltpu.VMEM((2048, 128), jnp.float32),
            pltpu.VMEM((2, 1024, 128), jnp.bfloat16),
            pltpu.VMEM((2, 128, 1024), jnp.float32),
            pltpu.SemaphoreType.DMA((2,)),
        ],
        compiler_params=pltpu.CompilerParams(vmem_limit_bytes=VMEM),
        cost_estimate=pl.CostEstimate(
            flops=40_000_000, bytes_accessed=6_000_000, transcendentals=0
        ),
        name="own",
    )(lengths, own, table, turns)


def fourier_kernel(
    fields,
    own_turned,
    other,
    table_north,
    turns,
    limits,
    table_ref,
    out_ref,
    table_south,
    rows,
    parts,
    bands,
    turned,
    out,
    sems,
):
    half_width = out.shape[2]
    slots = turns.shape[2] // 128
    lev = lax.axis_index("lev")
    start = lev * half_width
    fetch = pltpu.make_async_copy(table_ref.at[1], table_south, sems.at[0])
    fetch.start()

    def multiply(lat, number, lines, beside=None):
        table = table_south if lat else table_north
        values = lax.dot_general(
            lines[...], table[0:BLOCK], NT, preferred_element_type=jnp.float32
        )
        tail = lax.dot_general(
            lines[(PIECES - 1) * fields :, :],
            table[BLOCK : BLOCK + 16],
            NT,
            preferred_element_type=jnp.float32,
        )
        if beside is not None:
            beside()
        level = pl.ds(pl.multiple_of((number ^ lev) * fields, 16), fields)
        column = lax.broadcasted_iota(jnp.int32, (1, BLOCK), 1) + start
        limit = limits[8 * lat : 8 * lat + 1]
        for piece in range(PIECES):
            out[lat, level, piece * BLOCK : piece * BLOCK + BLOCK] = jnp.where(
                column + piece * BLOCK < limit, values[piece * fields : piece * fields + fields], 0.0
            ).astype(jnp.bfloat16)
        kept = column[:, 0:16] + PIECES * BLOCK < limit[:, 0:16]
        out[lat, level, PIECES * BLOCK :] = jnp.where(kept, tail, 0.0)[
            :, 0 : half_width - PIECES * BLOCK
        ].astype(jnp.bfloat16)
        copy = pltpu.make_async_copy(
            out.at[lat, level], out_ref.at[lat, level], sems.at[1 + 2 * lat + number]
        )
        copy.start()
        return copy

    def turn_other(lat):
        for slot in range(slots):
            turn(bands.at[lat], turns, lat, slot, turned.at[lat])

    def open_other():
        unpack(other, rows, parts, (bands.at[0], bands.at[1]))
        turn_other(0)

    copies = [
        multiply(0, 0, own_turned.at[0], open_other),
        multiply(0, 1, turned.at[0], lambda: turn_other(1)),
    ]
    fetch.wait()
    copies += [multiply(1, 0, own_turned.at[1]), multiply(1, 1, turned.at[1])]
    for copy in copies:
        copy.wait()


def fourier_call(own_turned, other, table_north, turns, limits, table, half_width, fields):
    shape = (2, 2 * fields, half_width)
    return pl.pallas_call(
        functools.partial(fourier_kernel, fields),
        out_shape=jax.ShapeDtypeStruct(shape, jnp.bfloat16),
        in_specs=[pl.BlockSpec(memory_space=pltpu.VMEM)] * 5
        + [pl.BlockSpec(memory_space=pl.ANY)],
        out_specs=pl.BlockSpec(memory_space=pl.ANY),
        scratch_shapes=[
            pltpu.VMEM(table_north.shape, jnp.bfloat16),
            pltpu.VMEM((2048, 128), jnp.float32),
            pltpu.VMEM((2, 1024, 128), jnp.bfloat16),
            pltpu.VMEM((2, 128, 1024), jnp.float32),
            pltpu.VMEM(own_turned.shape, jnp.bfloat16),
            pltpu.VMEM(shape, jnp.bfloat16),
            pltpu.SemaphoreType.DMA((5,)),
        ],
        compiler_params=pltpu.CompilerParams(vmem_limit_bytes=VMEM),
        name="fourier",
    )(own_turned, other, table_north, turns, limits, table)


def on_device(spectra, legendre, wave_slots, row_length):
    slots = spectra.shape[0]
    fields = spectra.shape[1] // 2
    total = wave_slots.shape[0]
    half_width = (4 * total + 16) // 2
    lev = lax.axis_index("lev").astype(jnp.int32)
    scalars = jnp.concatenate([row_length, lev[None]])
    waves = wave_slots.reshape(total // slots, slots).T.reshape(1, total)
    sent = legendre_call(wave_slots, legendre, spectra)
    arrived = lax.all_to_all(sent, "wave", split_axis=0, concat_axis=0, tiled=True)
    table, turns = table_call(scalars, waves, half_width)
    arrived, table, turns = lax.optimization_barrier((arrived, table, turns))
    other = lax.ppermute(arrived, "lev", [(0, 1), (1, 0)])
    own_turned, table_north, turns, limits = own_call(row_length, arrived, table, turns, fields)
    return fourier_call(
        own_turned, other, table_north, turns, limits, table, half_width, fields
    )


def solution(mesh):
    placed = (P("wave", "lev", None), P("wave", None, None), P(), P("wave"))
    return jax.shard_map(
        on_device, mesh=mesh, in_specs=placed, out_specs=P("wave", None, "lev"), check_vma=False
    )
```

```python
import functools
import math

import jax
import jax.numpy as jnp
import numpy as np
from jax import lax
from jax.experimental import pallas as pl
from jax.experimental.pallas import tpu as pltpu
from jax.sharding import PartitionSpec as P

BLOCK = 512
PIECES = 5
VMEM = 48 << 20
NT = (((1,), (1,)), ((), ()))
CHUNK = 256


def exchange_order():
    x, y, z = np.meshgrid(np.arange(4), np.arange(4), np.arange(8), indexing="ij")
    hops = np.minimum(x, 4 - x) + np.minimum(y, 4 - y) + np.minimum(z, 8 - z)
    return np.argsort(-hops.reshape(-1), kind="stable")


def legendre_kernel(
    waves_ref,
    order_ref,
    legendre,
    spectra,
    sent,
    waves,
    order,
    tables,
    spectrum,
    sums,
    rows,
    sems,
    extra,
):
    slots, columns, degrees = spectrum.shape
    lats = tables.shape[1]
    steps = degrees // CHUNK + 1
    copies = [
        (
            pltpu.make_async_copy(legendre.at[slot], tables.at[slot], sems.at[slot, 0]),
            pltpu.make_async_copy(spectra.at[slot], spectrum.at[slot], sems.at[slot, 1]),
        )
        for slot in range(slots)
    ]
    fetch = pltpu.make_async_copy(waves_ref, waves, extra.at[0])
    fetch.start()
    fetch_order = pltpu.make_async_copy(order_ref, order, extra.at[1])
    fetch_order.start()
    for both in copies:
        for copy in both:
            copy.start()
    first = lax.axis_index("wave") * slots
    sums[...] = jnp.zeros_like(sums)
    fetch.wait()
    for pair in range(slots // 2):
        for slot in (2 * pair, 2 * pair + 1):
            for copy in copies[slot]:
                copy.wait()
        wave = waves[first + 2 * pair]
        skipped = wave // CHUNK
        split = steps - 1 - skipped
        for step in range(steps):
            later = step >= split
            slot = 2 * pair + later.astype(jnp.int32)
            start = pl.multiple_of(jnp.where(later, step - 1, skipped + step) * CHUNK, CHUNK)
            number = jnp.where(later, degrees - 1 - wave, wave)
            degree = lax.broadcasted_iota(jnp.int32, (1, CHUNK), 1) + start
            mask = jnp.where(degree >= number // 64 * 64, 1.0, 0.0)
            signed = jnp.where((degree - number) % 2 == 0, mask, -mask).astype(jnp.bfloat16)
            own = spectrum[slot, :, pl.ds(start, CHUNK)]
            both = lax.dot_general(
                jnp.concatenate([own * mask.astype(jnp.bfloat16), own * signed], axis=0),
                tables[slot, :, pl.ds(start, CHUNK)],
                NT,
                preferred_element_type=jnp.float32,
            )
            at = pl.ds(pl.multiple_of(slot * columns, 32), columns)
            sums[at, 0:lats] += both[0:columns]
            sums[at, lats:] += both[columns:]
        if pair == 0:
            fetch_order.wait()
        done = [pair * 2 * columns // 128, (pair + 1) * 2 * columns // 128]
        for part in range(done[0], done[1] if pair < slots // 2 - 1 else 8):
            rows[pl.ds(part, 2 * lats, stride=8), :] = lax.dot_general(
                order[...],
                sums[part * 128 : part * 128 + 128].astype(jnp.bfloat16),
                NT,
                preferred_element_type=jnp.float32,
            )
    sent[...] = rows[...].astype(jnp.bfloat16).reshape(sent.shape)


def legendre_call(waves, legendre, spectra):
    slots, lats, degrees = legendre.shape
    columns = spectra.shape[1]
    lines = (2 * exchange_order()[:, None] + np.arange(2)).reshape(-1)
    order = jnp.asarray(lines[:, None] == np.arange(2 * lats), jnp.bfloat16)
    return pl.pallas_call(
        legendre_kernel,
        out_shape=jax.ShapeDtypeStruct((128, 16, 128), jnp.bfloat16),
        in_specs=[pl.BlockSpec(memory_space=pl.ANY)] * 4,
        out_specs=pl.BlockSpec(memory_space=pltpu.VMEM),
        scratch_shapes=[
            pltpu.SMEM(waves.shape, jnp.int32),
            pltpu.VMEM(order.shape, jnp.bfloat16),
            pltpu.VMEM((slots, lats, degrees), jnp.bfloat16),
            pltpu.VMEM((slots, columns, degrees), jnp.bfloat16),
            pltpu.VMEM((1024, 2 * lats), jnp.float32),
            pltpu.VMEM((2048, 128), jnp.float32),
            pltpu.SemaphoreType.DMA((slots, 2)),
            pltpu.SemaphoreType.DMA((2,)),
        ],
        compiler_params=pltpu.CompilerParams(vmem_limit_bytes=60 << 20),
        name="legendre",
    )(waves, order, legendre, spectra)


def circle(waves, starts, length):
    whole = waves * starts
    turns = jnp.floor(whole * (1.0 / length))
    phase = whole - turns * length
    phase = jnp.where(phase < 0.0, phase + length, phase)
    phase = jnp.where(phase >= length, phase - length, phase)
    angle = (2.0 * math.pi) * phase / length
    return jnp.cos(angle), jnp.sin(angle)


def table_kernel(half_width, scalars, waves_ref, table, turns, coarse_cos, coarse_sin):
    total = waves_ref.shape[1]
    lat = pl.program_id(0)
    row_length = scalars[lat]
    length = jnp.full((1, total), row_length, jnp.int32).astype(jnp.float32)
    wave = waves_ref[...]
    waves = wave.astype(jnp.float32)
    start = scalars[2] * half_width
    weight = jnp.where(wave == 0, 1.0, 2.0)
    weight = jnp.where(wave <= (row_length - 1) // 2, weight, 0.0)
    eight = lax.broadcasted_iota(jnp.int32, (8, total), 0)
    cos_a, sin_a = circle(waves, (eight * BLOCK + start).astype(jnp.float32), length)
    last = lax.broadcasted_iota(jnp.int32, (8, total), 0) == 7
    turns[0, 0:8] = jnp.where(last, length, cos_a * weight)
    turns[0, 8:16] = sin_a * weight
    coarse = lax.broadcasted_iota(jnp.int32, coarse_cos.shape, 0) * 16
    coarse_cos[...], coarse_sin[...] = circle(waves, coarse.astype(jnp.float32), length)
    fine = lax.broadcasted_iota(jnp.int32, (16, total), 0)
    fine_cos, fine_sin = circle(waves, fine.astype(jnp.float32), length)

    @pl.loop(0, table.shape[1] // 16)
    def _(step):
        cos_u, sin_u = coarse_cos[pl.ds(step, 1), :], coarse_sin[pl.ds(step, 1), :]
        at = pl.ds(pl.multiple_of(step * 16, 16), 16)
        table[0, at, 0:total] = (cos_u * fine_cos - sin_u * fine_sin).astype(jnp.bfloat16)
        table[0, at, total:] = (-(sin_u * fine_cos + cos_u * fine_sin)).astype(jnp.bfloat16)


def table_call(scalars, waves, half_width):
    total = waves.shape[1]
    rows = BLOCK + 16
    return pl.pallas_call(
        functools.partial(table_kernel, half_width),
        out_shape=[
            jax.ShapeDtypeStruct((2, rows, 2 * total), jnp.bfloat16),
            jax.ShapeDtypeStruct((2, 16, total), jnp.float32),
        ],
        grid_spec=pltpu.PrefetchScalarGridSpec(
            num_scalar_prefetch=1,
            grid=(2,),
            in_specs=[pl.BlockSpec((1, total), lambda l, s: (0, 0))],
            out_specs=[
                pl.BlockSpec((1, rows, 2 * total), lambda l, s: (l, 0, 0)),
                pl.BlockSpec((1, 16, total), lambda l, s: (l, 0, 0)),
            ],
            scratch_shapes=[pltpu.VMEM((40, total), jnp.float32)] * 2,
        ),
        compiler_params=pltpu.CompilerParams(vmem_limit_bytes=32 << 20),
        cost_estimate=pl.CostEstimate(
            flops=20_000_000, bytes_accessed=6_000_000, transcendentals=400_000
        ),
        name="tables",
    )(scalars, waves)


def unpack(arrived, rows, parts, keep):
    rows[...] = arrived[...].astype(jnp.float32).reshape(2048, 128)
    i = lax.broadcasted_iota(jnp.int32, (128, 128), 0)
    j = lax.broadcasted_iota(jnp.int32, (128, 128), 1)
    source = i // 32 * 32 + jnp.where(i % 32 < 16, 2 * (i % 16), 2 * (i % 16) + 1)
    sort = jnp.where(source == j, 1.0, 0.0).astype(jnp.bfloat16)
    for lat in (0, 1):
        for place in range(8):
            parts[lat, place * 128 : place * 128 + 128] = rows[
                pl.ds(lat * 8 + place, 128, stride=16), :
            ].astype(jnp.bfloat16)
        keep[lat][...] = lax.dot_general(sort, parts[lat], NT, preferred_element_type=jnp.float32)


def turn(bands, turns, lat, slot, turned):
    total = turns.shape[2]
    fields = turned.shape[0] // PIECES
    at = pl.ds(pl.multiple_of(slot * 128, 128), 128)
    behind = pl.ds(pl.multiple_of(total + slot * 128, 128), 128)
    for third in range(fields // 16):
        group = slot * (fields // 16) + third
        lanes = pl.ds(pl.multiple_of(group // 4 * 128, 128), 128)
        base = pl.multiple_of(group % 4 * 32, 32)
        real = bands[pl.ds(base, 16), lanes]
        imag = bands[pl.ds(base + 16, 16), lanes]
        for piece in range(PIECES):
            cos_a = turns[lat, piece : piece + 1, at]
            sin_a = turns[lat, 8 + piece : 9 + piece, at]
            row = piece * fields + third * 16
            turned[row : row + 16, at] = (real * cos_a - imag * sin_a).astype(jnp.bfloat16)
            turned[row : row + 16, behind] = (real * sin_a + imag * cos_a).astype(jnp.bfloat16)


def own_kernel(
    own, table_ref, turns_ref, turned, table, turns, rows, parts, bands, sems
):
    fetch = [
        pltpu.make_async_copy(turns_ref, turns, sems.at[0]),
        pltpu.make_async_copy(table_ref.at[0], table, sems.at[1]),
    ]
    for copy in fetch:
        copy.start()
    unpack(own, rows, parts, (bands.at[0], bands.at[1]))
    fetch[0].wait()

    @pl.loop(0, turns.shape[2] // 128)
    def _(slot):
        for lat in (0, 1):
            turn(bands.at[lat], turns, lat, slot, turned.at[lat])

    fetch[1].wait()


def own_call(own, table, turns, fields):
    return pl.pallas_call(
        own_kernel,
        out_shape=[
            jax.ShapeDtypeStruct((2, PIECES * fields, table.shape[2]), jnp.bfloat16),
            jax.ShapeDtypeStruct(table.shape[1:], jnp.bfloat16),
            jax.ShapeDtypeStruct(turns.shape, jnp.float32),
        ],
        in_specs=[
            pl.BlockSpec(memory_space=pltpu.VMEM),
            pl.BlockSpec(memory_space=pl.ANY),
            pl.BlockSpec(memory_space=pl.ANY),
        ],
        out_specs=[pl.BlockSpec(memory_space=pltpu.VMEM)] * 3,
        scratch_shapes=[
            pltpu.VMEM((2048, 128), jnp.float32),
            pltpu.VMEM((2, 1024, 128), jnp.bfloat16),
            pltpu.VMEM((2, 128, 1024), jnp.float32),
            pltpu.SemaphoreType.DMA((2,)),
        ],
        compiler_params=pltpu.CompilerParams(vmem_limit_bytes=VMEM),
        cost_estimate=pl.CostEstimate(
            flops=40_000_000, bytes_accessed=6_000_000, transcendentals=0
        ),
        name="own",
    )(own, table, turns)


def fourier_kernel(
    fields,
    own_turned,
    other,
    table_north,
    turns,
    table_ref,
    out_ref,
    table_south,
    rows,
    parts,
    bands,
    turned,
    out,
    sems,
):
    half_width = out.shape[2]
    slots = turns.shape[2] // 128
    lev = lax.axis_index("lev")
    start = lev * half_width
    fetch = pltpu.make_async_copy(table_ref.at[1], table_south, sems.at[0])
    fetch.start()

    def multiply(lat, number, lines, beside=None):
        table = table_south if lat else table_north
        values = lax.dot_general(
            lines[...], table[0:BLOCK], NT, preferred_element_type=jnp.float32
        )
        tail = lax.dot_general(
            lines[(PIECES - 1) * fields :, :],
            table[BLOCK : BLOCK + 16],
            NT,
            preferred_element_type=jnp.float32,
        )
        if beside is not None:
            beside()
        level = pl.ds(pl.multiple_of((number ^ lev) * fields, 16), fields)
        column = lax.broadcasted_iota(jnp.int32, (1, BLOCK), 1) + start
        limit = turns[lat, 7:8, 0:BLOCK].astype(jnp.int32)
        for piece in range(PIECES):
            out[lat, level, piece * BLOCK : piece * BLOCK + BLOCK] = jnp.where(
                column + piece * BLOCK < limit, values[piece * fields : piece * fields + fields], 0.0
            ).astype(jnp.bfloat16)
        kept = column[:, 0:16] + PIECES * BLOCK < limit[:, 0:16]
        out[lat, level, PIECES * BLOCK :] = jnp.where(kept, tail, 0.0)[
            :, 0 : half_width - PIECES * BLOCK
        ].astype(jnp.bfloat16)
        copy = pltpu.make_async_copy(
            out.at[lat, level], out_ref.at[lat, level], sems.at[1 + 2 * lat + number]
        )
        copy.start()
        return copy

    def turn_other(lat):
        for slot in range(slots):
            turn(bands.at[lat], turns, lat, slot, turned.at[lat])

    def open_other():
        unpack(other, rows, parts, (bands.at[0], bands.at[1]))
        turn_other(0)

    copies = [
        multiply(0, 0, own_turned.at[0], open_other),
        multiply(0, 1, turned.at[0], lambda: turn_other(1)),
    ]
    fetch.wait()
    copies += [multiply(1, 0, own_turned.at[1]), multiply(1, 1, turned.at[1])]
    for copy in copies:
        copy.wait()


def fourier_call(own_turned, other, table_north, turns, table, half_width, fields):
    shape = (2, 2 * fields, half_width)
    return pl.pallas_call(
        functools.partial(fourier_kernel, fields),
        out_shape=jax.ShapeDtypeStruct(shape, jnp.bfloat16),
        in_specs=[pl.BlockSpec(memory_space=pltpu.VMEM)] * 4
        + [pl.BlockSpec(memory_space=pl.ANY)],
        out_specs=pl.BlockSpec(memory_space=pl.ANY),
        scratch_shapes=[
            pltpu.VMEM(table_north.shape, jnp.bfloat16),
            pltpu.VMEM((2048, 128), jnp.float32),
            pltpu.VMEM((2, 1024, 128), jnp.bfloat16),
            pltpu.VMEM((2, 128, 1024), jnp.float32),
            pltpu.VMEM(own_turned.shape, jnp.bfloat16),
            pltpu.VMEM(shape, jnp.bfloat16),
            pltpu.SemaphoreType.DMA((5,)),
        ],
        compiler_params=pltpu.CompilerParams(vmem_limit_bytes=VMEM),
        name="fourier",
    )(own_turned, other, table_north, turns, table)


def on_device(spectra, legendre, wave_slots, row_length):
    slots = spectra.shape[0]
    fields = spectra.shape[1] // 2
    total = wave_slots.shape[0]
    half_width = (4 * total + 16) // 2
    lev = lax.axis_index("lev").astype(jnp.int32)
    scalars = jnp.concatenate([row_length, lev[None]])
    order = exchange_order()
    waves = wave_slots.reshape(total // slots, slots)[order].T.reshape(1, total)
    sent = legendre_call(wave_slots, legendre, spectra)
    arrived = lax.all_to_all(
        sent,
        "wave",
        split_axis=0,
        concat_axis=0,
        axis_index_groups=[[int(chip) for chip in order]],
        tiled=True,
    )
    table, turns = table_call(scalars, waves, half_width)
    arrived, table, turns = lax.optimization_barrier((arrived, table, turns))
    other = lax.ppermute(arrived, "lev", [(0, 1), (1, 0)])
    own_turned, table_north, turns = own_call(arrived, table, turns, fields)
    return fourier_call(own_turned, other, table_north, turns, table, half_width, fields)


def solution(mesh):
    placed = (P("wave", "lev", None), P("wave", None, None), P(), P("wave"))
    return jax.shard_map(
        on_device, mesh=mesh, in_specs=placed, out_specs=P("wave", None, "lev"), check_vma=False
    )
```

```python
import functools
import math

import jax
import jax.numpy as jnp
import numpy as np
from jax import lax
from jax.experimental import pallas as pl
from jax.experimental.pallas import tpu as pltpu
from jax.sharding import PartitionSpec as P

BLOCK = 512
PIECES = 5
VMEM = 48 << 20
NT = (((1,), (1,)), ((), ()))
CHUNK = 256


def exchange_order():
    x, y, z = np.meshgrid(np.arange(4), np.arange(4), np.arange(8), indexing="ij")
    hops = np.minimum(x, 4 - x) + np.minimum(y, 4 - y) + np.minimum(z, 8 - z)
    return np.argsort(-hops.reshape(-1), kind="stable")


def legendre_kernel(
    waves_ref,
    order_ref,
    legendre,
    spectra,
    sent,
    waves,
    order,
    tables,
    spectrum,
    sums,
    rows,
    sems,
    extra,
):
    slots, columns, degrees = spectrum.shape
    lats = tables.shape[1]
    steps = degrees // CHUNK + 1
    copies = [
        (
            pltpu.make_async_copy(legendre.at[slot], tables.at[slot], sems.at[slot, 0]),
            pltpu.make_async_copy(spectra.at[slot], spectrum.at[slot], sems.at[slot, 1]),
        )
        for slot in range(slots)
    ]
    fetch = pltpu.make_async_copy(waves_ref, waves, extra.at[0])
    fetch.start()
    fetch_order = pltpu.make_async_copy(order_ref, order, extra.at[1])
    fetch_order.start()
    for both in copies:
        for copy in both:
            copy.start()
    first = lax.axis_index("wave") * slots
    sums[...] = jnp.zeros_like(sums)
    fetch.wait()
    for pair in range(slots // 2):
        for slot in (2 * pair, 2 * pair + 1):
            for copy in copies[slot]:
                copy.wait()
        wave = waves[first + 2 * pair]
        skipped = wave // CHUNK
        split = steps - 1 - skipped
        for step in range(steps):
            later = step >= split
            slot = 2 * pair + later.astype(jnp.int32)
            start = pl.multiple_of(jnp.where(later, step - 1, skipped + step) * CHUNK, CHUNK)
            number = jnp.where(later, degrees - 1 - wave, wave)
            degree = lax.broadcasted_iota(jnp.int32, (1, CHUNK), 1) + start
            mask = jnp.where(degree >= number // 64 * 64, 1.0, 0.0)
            signed = jnp.where((degree - number) % 2 == 0, mask, -mask).astype(jnp.bfloat16)
            own = spectrum[slot, :, pl.ds(start, CHUNK)]
            both = lax.dot_general(
                jnp.concatenate([own * mask.astype(jnp.bfloat16), own * signed], axis=0),
                tables[slot, :, pl.ds(start, CHUNK)],
                NT,
                preferred_element_type=jnp.float32,
            )
            at = pl.ds(pl.multiple_of(slot * columns, 32), columns)
            sums[at, 0:lats] += both[0:columns]
            sums[at, lats:] += both[columns:]
    fetch_order.wait()
    for part in range(8):
        rows[pl.ds(part, 2 * lats, stride=8), :] = lax.dot_general(
            order[...],
            sums[part * 128 : part * 128 + 128].astype(jnp.bfloat16),
            NT,
            preferred_element_type=jnp.float32,
        )
    sent[...] = rows[...].astype(jnp.bfloat16).reshape(sent.shape)


def legendre_call(waves, legendre, spectra):
    slots, lats, degrees = legendre.shape
    columns = spectra.shape[1]
    lines = (2 * exchange_order()[:, None] + np.arange(2)).reshape(-1)
    order = jnp.asarray(lines[:, None] == np.arange(2 * lats), jnp.bfloat16)
    return pl.pallas_call(
        legendre_kernel,
        out_shape=jax.ShapeDtypeStruct((128, 16, 128), jnp.bfloat16),
        in_specs=[pl.BlockSpec(memory_space=pl.ANY)] * 4,
        out_specs=pl.BlockSpec(memory_space=pltpu.VMEM),
        scratch_shapes=[
            pltpu.SMEM(waves.shape, jnp.int32),
            pltpu.VMEM(order.shape, jnp.bfloat16),
            pltpu.VMEM((slots, lats, degrees), jnp.bfloat16),
            pltpu.VMEM((slots, columns, degrees), jnp.bfloat16),
            pltpu.VMEM((1024, 2 * lats), jnp.float32),
            pltpu.VMEM((2048, 128), jnp.float32),
            pltpu.SemaphoreType.DMA((slots, 2)),
            pltpu.SemaphoreType.DMA((2,)),
        ],
        compiler_params=pltpu.CompilerParams(vmem_limit_bytes=60 << 20),
        name="legendre",
    )(waves, order, legendre, spectra)


def circle(waves, starts, length):
    whole = waves * starts
    turns = jnp.floor(whole * (1.0 / length))
    phase = whole - turns * length
    phase = jnp.where(phase < 0.0, phase + length, phase)
    phase = jnp.where(phase >= length, phase - length, phase)
    angle = (2.0 * math.pi) * phase / length
    return jnp.cos(angle), jnp.sin(angle)


def table_kernel(half_width, scalars, waves_ref, table, turns, coarse_cos, coarse_sin):
    total = waves_ref.shape[1]
    lat = pl.program_id(0)
    row_length = scalars[lat]
    length = jnp.full((1, total), row_length, jnp.int32).astype(jnp.float32)
    wave = waves_ref[...]
    waves = wave.astype(jnp.float32)
    start = scalars[2] * half_width
    weight = jnp.where(wave == 0, 1.0, 2.0)
    weight = jnp.where(wave <= (row_length - 1) // 2, weight, 0.0)
    eight = lax.broadcasted_iota(jnp.int32, (8, total), 0)
    cos_a, sin_a = circle(waves, (eight * BLOCK + start).astype(jnp.float32), length)
    last = lax.broadcasted_iota(jnp.int32, (8, total), 0) == 7
    turns[0, 0:8] = jnp.where(last, length, cos_a * weight)
    turns[0, 8:16] = sin_a * weight
    coarse = lax.broadcasted_iota(jnp.int32, coarse_cos.shape, 0) * 16
    coarse_cos[...], coarse_sin[...] = circle(waves, coarse.astype(jnp.float32), length)
    fine = lax.broadcasted_iota(jnp.int32, (16, total), 0)
    fine_cos, fine_sin = circle(waves, fine.astype(jnp.float32), length)

    @pl.loop(0, table.shape[1] // 16)
    def _(step):
        cos_u, sin_u = coarse_cos[pl.ds(step, 1), :], coarse_sin[pl.ds(step, 1), :]
        at = pl.ds(pl.multiple_of(step * 16, 16), 16)
        table[0, at, 0:total] = (cos_u * fine_cos - sin_u * fine_sin).astype(jnp.bfloat16)
        table[0, at, total:] = (-(sin_u * fine_cos + cos_u * fine_sin)).astype(jnp.bfloat16)


def table_call(scalars, waves, half_width):
    total = waves.shape[1]
    rows = BLOCK + 16
    return pl.pallas_call(
        functools.partial(table_kernel, half_width),
        out_shape=[
            jax.ShapeDtypeStruct((2, rows, 2 * total), jnp.bfloat16),
            jax.ShapeDtypeStruct((2, 16, total), jnp.float32),
        ],
        grid_spec=pltpu.PrefetchScalarGridSpec(
            num_scalar_prefetch=1,
            grid=(2,),
            in_specs=[pl.BlockSpec((1, total), lambda l, s: (0, 0))],
            out_specs=[
                pl.BlockSpec((1, rows, 2 * total), lambda l, s: (l, 0, 0)),
                pl.BlockSpec((1, 16, total), lambda l, s: (l, 0, 0)),
            ],
            scratch_shapes=[pltpu.VMEM((40, total), jnp.float32)] * 2,
        ),
        compiler_params=pltpu.CompilerParams(vmem_limit_bytes=32 << 20),
        cost_estimate=pl.CostEstimate(
            flops=20_000_000, bytes_accessed=6_000_000, transcendentals=400_000
        ),
        name="tables",
    )(scalars, waves)


def unpack(arrived, rows, parts, keep):
    rows[...] = arrived[...].astype(jnp.float32).reshape(2048, 128)
    i = lax.broadcasted_iota(jnp.int32, (128, 128), 0)
    j = lax.broadcasted_iota(jnp.int32, (128, 128), 1)
    source = i // 32 * 32 + jnp.where(i % 32 < 16, 2 * (i % 16), 2 * (i % 16) + 1)
    sort = jnp.where(source == j, 1.0, 0.0).astype(jnp.bfloat16)
    for lat in (0, 1):
        for place in range(8):
            parts[lat, place * 128 : place * 128 + 128] = rows[
                pl.ds(lat * 8 + place, 128, stride=16), :
            ].astype(jnp.bfloat16)
        keep[lat][...] = lax.dot_general(sort, parts[lat], NT, preferred_element_type=jnp.float32)


def turn(bands, turns, lat, slot, turned):
    total = turns.shape[2]
    fields = turned.shape[0] // PIECES
    at = pl.ds(pl.multiple_of(slot * 128, 128), 128)
    behind = pl.ds(pl.multiple_of(total + slot * 128, 128), 128)
    for third in range(fields // 16):
        group = slot * (fields // 16) + third
        lanes = pl.ds(pl.multiple_of(group // 4 * 128, 128), 128)
        base = pl.multiple_of(group % 4 * 32, 32)
        real = bands[pl.ds(base, 16), lanes]
        imag = bands[pl.ds(base + 16, 16), lanes]
        for piece in range(PIECES):
            cos_a = turns[lat, piece : piece + 1, at]
            sin_a = turns[lat, 8 + piece : 9 + piece, at]
            row = piece * fields + third * 16
            turned[row : row + 16, at] = (real * cos_a - imag * sin_a).astype(jnp.bfloat16)
            turned[row : row + 16, behind] = (real * sin_a + imag * cos_a).astype(jnp.bfloat16)


def own_kernel(
    own, table_ref, turns_ref, turned, table, turns, rows, parts, bands, sems
):
    fetch = [
        pltpu.make_async_copy(turns_ref, turns, sems.at[0]),
        pltpu.make_async_copy(table_ref.at[0], table, sems.at[1]),
    ]
    for copy in fetch:
        copy.start()
    unpack(own, rows, parts, (bands.at[0], bands.at[1]))
    fetch[0].wait()

    @pl.loop(0, turns.shape[2] // 128)
    def _(slot):
        for lat in (0, 1):
            turn(bands.at[lat], turns, lat, slot, turned.at[lat])

    fetch[1].wait()


def own_call(own, table, turns, fields):
    return pl.pallas_call(
        own_kernel,
        out_shape=[
            jax.ShapeDtypeStruct((2, PIECES * fields, table.shape[2]), jnp.bfloat16),
            jax.ShapeDtypeStruct(table.shape[1:], jnp.bfloat16),
            jax.ShapeDtypeStruct(turns.shape, jnp.float32),
        ],
        in_specs=[
            pl.BlockSpec(memory_space=pltpu.VMEM),
            pl.BlockSpec(memory_space=pl.ANY),
            pl.BlockSpec(memory_space=pl.ANY),
        ],
        out_specs=[pl.BlockSpec(memory_space=pltpu.VMEM)] * 3,
        scratch_shapes=[
            pltpu.VMEM((2048, 128), jnp.float32),
            pltpu.VMEM((2, 1024, 128), jnp.bfloat16),
            pltpu.VMEM((2, 128, 1024), jnp.float32),
            pltpu.SemaphoreType.DMA((2,)),
        ],
        compiler_params=pltpu.CompilerParams(vmem_limit_bytes=VMEM),
        cost_estimate=pl.CostEstimate(
            flops=40_000_000, bytes_accessed=6_000_000, transcendentals=0
        ),
        name="own",
    )(own, table, turns)


def fourier_kernel(
    fields,
    own_turned,
    other,
    table_north,
    turns,
    table_ref,
    out_ref,
    table_south,
    rows,
    parts,
    bands,
    turned,
    out,
    sems,
):
    half_width = out.shape[2]
    slots = turns.shape[2] // 128
    lev = lax.axis_index("lev")
    start = lev * half_width
    fetch = pltpu.make_async_copy(table_ref.at[1], table_south, sems.at[0])
    fetch.start()

    def multiply(lat, number, lines, beside=None):
        table = table_south if lat else table_north
        values = lax.dot_general(
            lines[...], table[0:BLOCK], NT, preferred_element_type=jnp.float32
        )
        tail = lax.dot_general(
            lines[(PIECES - 1) * fields :, :],
            table[BLOCK : BLOCK + 16],
            NT,
            preferred_element_type=jnp.float32,
        )
        if beside is not None:
            beside()
        level = pl.ds(pl.multiple_of((number ^ lev) * fields, 16), fields)
        column = lax.broadcasted_iota(jnp.int32, (1, BLOCK), 1) + start
        limit = turns[lat, 7:8, 0:BLOCK].astype(jnp.int32)
        for piece in range(PIECES):
            out[lat, level, piece * BLOCK : piece * BLOCK + BLOCK] = jnp.where(
                column + piece * BLOCK < limit, values[piece * fields : piece * fields + fields], 0.0
            ).astype(jnp.bfloat16)
        kept = column[:, 0:16] + PIECES * BLOCK < limit[:, 0:16]
        out[lat, level, PIECES * BLOCK :] = jnp.where(kept, tail, 0.0)[
            :, 0 : half_width - PIECES * BLOCK
        ].astype(jnp.bfloat16)
        copy = pltpu.make_async_copy(
            out.at[lat, level], out_ref.at[lat, level], sems.at[1 + 2 * lat + number]
        )
        copy.start()
        return copy

    def turn_other(lat):
        for slot in range(slots):
            turn(bands.at[lat], turns, lat, slot, turned.at[lat])

    def open_other():
        unpack(other, rows, parts, (bands.at[0], bands.at[1]))
        turn_other(0)

    copies = [
        multiply(0, 0, own_turned.at[0], open_other),
        multiply(0, 1, turned.at[0], lambda: turn_other(1)),
    ]
    fetch.wait()
    copies += [multiply(1, 0, own_turned.at[1]), multiply(1, 1, turned.at[1])]
    for copy in copies:
        copy.wait()


def fourier_call(own_turned, other, table_north, turns, table, half_width, fields):
    shape = (2, 2 * fields, half_width)
    return pl.pallas_call(
        functools.partial(fourier_kernel, fields),
        out_shape=jax.ShapeDtypeStruct(shape, jnp.bfloat16),
        in_specs=[pl.BlockSpec(memory_space=pltpu.VMEM)] * 4
        + [pl.BlockSpec(memory_space=pl.ANY)],
        out_specs=pl.BlockSpec(memory_space=pl.ANY),
        scratch_shapes=[
            pltpu.VMEM(table_north.shape, jnp.bfloat16),
            pltpu.VMEM((2048, 128), jnp.float32),
            pltpu.VMEM((2, 1024, 128), jnp.bfloat16),
            pltpu.VMEM((2, 128, 1024), jnp.float32),
            pltpu.VMEM(own_turned.shape, jnp.bfloat16),
            pltpu.VMEM(shape, jnp.bfloat16),
            pltpu.SemaphoreType.DMA((5,)),
        ],
        compiler_params=pltpu.CompilerParams(vmem_limit_bytes=VMEM),
        name="fourier",
    )(own_turned, other, table_north, turns, table)


def on_device(spectra, legendre, wave_slots, row_length):
    slots = spectra.shape[0]
    fields = spectra.shape[1] // 2
    total = wave_slots.shape[0]
    half_width = (4 * total + 16) // 2
    lev = lax.axis_index("lev").astype(jnp.int32)
    scalars = jnp.concatenate([row_length, lev[None]])
    order = exchange_order()
    waves = wave_slots.reshape(total // slots, slots)[order].T.reshape(1, total)
    sent = legendre_call(wave_slots, legendre, spectra)
    arrived = lax.all_to_all(
        sent,
        "wave",
        split_axis=0,
        concat_axis=0,
        axis_index_groups=[[int(chip) for chip in order]],
        tiled=True,
    )
    table, turns = table_call(scalars, waves, half_width)
    arrived, table, turns = lax.optimization_barrier((arrived, table, turns))
    other = lax.ppermute(arrived, "lev", [(0, 1), (1, 0)])
    own_turned, table_north, turns = own_call(arrived, table, turns, fields)
    return fourier_call(own_turned, other, table_north, turns, table, half_width, fields)


def solution(mesh):
    placed = (P("wave", "lev", None), P("wave", None, None), P(), P("wave"))
    return jax.shard_map(
        on_device, mesh=mesh, in_specs=placed, out_specs=P("wave", None, "lev"), check_vma=False
    )
```

```python
import functools
import math

import jax
import jax.numpy as jnp
import numpy as np
from jax import lax
from jax.experimental import pallas as pl
from jax.experimental.pallas import tpu as pltpu
from jax.sharding import PartitionSpec as P

BLOCK = 512
PIECES = 5
VMEM = 48 << 20
NT = (((1,), (1,)), ((), ()))
CHUNK = 256


def exchange_order():
    x, y, z = np.meshgrid(np.arange(4), np.arange(4), np.arange(8), indexing="ij")
    hops = np.minimum(x, 4 - x) + np.minimum(y, 4 - y) + np.minimum(z, 8 - z)
    return np.argsort(-hops.reshape(-1), kind="stable")


def legendre_kernel(
    waves_ref,
    order_ref,
    legendre,
    spectra,
    sent,
    waves,
    order,
    tables,
    spectrum,
    sums,
    rows,
    sems,
    extra,
):
    slots, columns, degrees = spectrum.shape
    lats = tables.shape[1]
    steps = degrees // CHUNK + 1
    copies = [
        (
            pltpu.make_async_copy(legendre.at[slot], tables.at[slot], sems.at[slot, 0]),
            pltpu.make_async_copy(spectra.at[slot], spectrum.at[slot], sems.at[slot, 1]),
        )
        for slot in range(slots)
    ]
    fetch = pltpu.make_async_copy(waves_ref, waves, extra.at[0])
    fetch.start()
    fetch_order = pltpu.make_async_copy(order_ref, order, extra.at[1])
    fetch_order.start()
    for both in copies:
        for copy in both:
            copy.start()
    first = lax.axis_index("wave") * slots
    sums[...] = jnp.zeros_like(sums)
    fetch.wait()
    for pair in range(slots // 2):
        for slot in (2 * pair, 2 * pair + 1):
            for copy in copies[slot]:
                copy.wait()
        wave = waves[first + 2 * pair]
        skipped = wave // CHUNK
        split = steps - 1 - skipped
        for step in range(steps):
            later = step >= split
            slot = 2 * pair + later.astype(jnp.int32)
            start = pl.multiple_of(jnp.where(later, step - 1, skipped + step) * CHUNK, CHUNK)
            number = jnp.where(later, degrees - 1 - wave, wave)
            degree = lax.broadcasted_iota(jnp.int32, (1, CHUNK), 1) + start
            mask = jnp.where(degree >= number // 64 * 64, 1.0, 0.0)
            signed = jnp.where((degree - number) % 2 == 0, mask, -mask).astype(jnp.bfloat16)
            own = spectrum[slot, :, pl.ds(start, CHUNK)]
            both = lax.dot_general(
                jnp.concatenate([own * mask.astype(jnp.bfloat16), own * signed], axis=0),
                tables[slot, :, pl.ds(start, CHUNK)],
                NT,
                preferred_element_type=jnp.float32,
            )
            at = pl.ds(pl.multiple_of(slot * columns, 32), columns)
            sums[at, 0:lats] += both[0:columns]
            sums[at, lats:] += both[columns:]
    fetch_order.wait()
    for part in range(8):
        rows[pl.ds(part, 2 * lats, stride=8), :] = lax.dot_general(
            order[...],
            sums[part * 128 : part * 128 + 128].astype(jnp.bfloat16),
            NT,
            preferred_element_type=jnp.float32,
        )
    sent[...] = rows[...].astype(jnp.bfloat16).reshape(sent.shape)


def legendre_call(waves, legendre, spectra):
    slots, lats, degrees = legendre.shape
    columns = spectra.shape[1]
    lines = (2 * exchange_order()[:, None] + np.arange(2)).reshape(-1)
    order = jnp.asarray(lines[:, None] == np.arange(2 * lats), jnp.bfloat16)
    return pl.pallas_call(
        legendre_kernel,
        out_shape=jax.ShapeDtypeStruct((128, 16, 128), jnp.bfloat16),
        in_specs=[pl.BlockSpec(memory_space=pl.ANY)] * 4,
        out_specs=pl.BlockSpec(memory_space=pltpu.VMEM),
        scratch_shapes=[
            pltpu.SMEM(waves.shape, jnp.int32),
            pltpu.VMEM(order.shape, jnp.bfloat16),
            pltpu.VMEM((slots, lats, degrees), jnp.bfloat16),
            pltpu.VMEM((slots, columns, degrees), jnp.bfloat16),
            pltpu.VMEM((1024, 2 * lats), jnp.float32),
            pltpu.VMEM((2048, 128), jnp.float32),
            pltpu.SemaphoreType.DMA((slots, 2)),
            pltpu.SemaphoreType.DMA((2,)),
        ],
        compiler_params=pltpu.CompilerParams(vmem_limit_bytes=60 << 20),
        name="legendre",
    )(waves, order, legendre, spectra)


def circle(waves, starts, length):
    whole = waves * starts
    turns = jnp.floor(whole * (1.0 / length))
    phase = whole - turns * length
    phase = jnp.where(phase < 0.0, phase + length, phase)
    phase = jnp.where(phase >= length, phase - length, phase)
    angle = (2.0 * math.pi) * phase / length
    return jnp.cos(angle), jnp.sin(angle)


def table_kernel(half_width, scalars, waves_ref, table, turns, coarse_cos, coarse_sin):
    total = waves_ref.shape[1]
    lat = pl.program_id(0)
    row_length = scalars[lat]
    length = jnp.full((1, total), row_length, jnp.int32).astype(jnp.float32)
    wave = waves_ref[...]
    waves = wave.astype(jnp.float32)
    start = scalars[2] * half_width
    weight = jnp.where(wave == 0, 1.0, 2.0)
    weight = jnp.where(wave <= (row_length - 1) // 2, weight, 0.0)
    eight = lax.broadcasted_iota(jnp.int32, (8, total), 0)
    cos_a, sin_a = circle(waves, (eight * BLOCK + start).astype(jnp.float32), length)
    last = lax.broadcasted_iota(jnp.int32, (8, total), 0) == 7
    turns[0, 0:8] = jnp.where(last, length, cos_a * weight)
    turns[0, 8:16] = sin_a * weight
    coarse = lax.broadcasted_iota(jnp.int32, coarse_cos.shape, 0) * 16
    coarse_cos[...], coarse_sin[...] = circle(waves, coarse.astype(jnp.float32), length)
    fine = lax.broadcasted_iota(jnp.int32, (16, total), 0)
    fine_cos, fine_sin = circle(waves, fine.astype(jnp.float32), length)

    @pl.loop(0, table.shape[1] // 16)
    def _(step):
        cos_u, sin_u = coarse_cos[pl.ds(step, 1), :], coarse_sin[pl.ds(step, 1), :]
        at = pl.ds(pl.multiple_of(step * 16, 16), 16)
        table[0, at, 0:total] = (cos_u * fine_cos - sin_u * fine_sin).astype(jnp.bfloat16)
        table[0, at, total:] = (-(sin_u * fine_cos + cos_u * fine_sin)).astype(jnp.bfloat16)


def table_call(scalars, waves, half_width):
    total = waves.shape[1]
    rows = BLOCK + 16
    return pl.pallas_call(
        functools.partial(table_kernel, half_width),
        out_shape=[
            jax.ShapeDtypeStruct((2, rows, 2 * total), jnp.bfloat16),
            jax.ShapeDtypeStruct((2, 16, total), jnp.float32),
        ],
        grid_spec=pltpu.PrefetchScalarGridSpec(
            num_scalar_prefetch=1,
            grid=(2,),
            in_specs=[pl.BlockSpec((1, total), lambda l, s: (0, 0))],
            out_specs=[
                pl.BlockSpec((1, rows, 2 * total), lambda l, s: (l, 0, 0)),
                pl.BlockSpec((1, 16, total), lambda l, s: (l, 0, 0)),
            ],
            scratch_shapes=[pltpu.VMEM((40, total), jnp.float32)] * 2,
        ),
        compiler_params=pltpu.CompilerParams(vmem_limit_bytes=32 << 20),
        cost_estimate=pl.CostEstimate(
            flops=20_000_000, bytes_accessed=6_000_000, transcendentals=400_000
        ),
        name="tables",
    )(scalars, waves)


def unpack(arrived, rows, parts, keep):
    rows[...] = arrived[...].astype(jnp.float32).reshape(2048, 128)
    i = lax.broadcasted_iota(jnp.int32, (128, 128), 0)
    j = lax.broadcasted_iota(jnp.int32, (128, 128), 1)
    source = i // 32 * 32 + jnp.where(i % 32 < 16, 2 * (i % 16), 2 * (i % 16) + 1)
    sort = jnp.where(source == j, 1.0, 0.0).astype(jnp.bfloat16)
    for lat in (0, 1):
        for place in range(8):
            parts[lat, place * 128 : place * 128 + 128] = rows[
                pl.ds(lat * 8 + place, 128, stride=16), :
            ].astype(jnp.bfloat16)
        keep[lat][...] = lax.dot_general(sort, parts[lat], NT, preferred_element_type=jnp.float32)


def turn(bands, turns, lat, slot, turned):
    total = turns.shape[2]
    fields = turned.shape[0] // PIECES
    at = pl.ds(pl.multiple_of(slot * 128, 128), 128)
    behind = pl.ds(pl.multiple_of(total + slot * 128, 128), 128)
    for third in range(fields // 16):
        group = slot * (fields // 16) + third
        lanes = pl.ds(pl.multiple_of(group // 4 * 128, 128), 128)
        base = pl.multiple_of(group % 4 * 32, 32)
        real = bands[pl.ds(base, 16), lanes]
        imag = bands[pl.ds(base + 16, 16), lanes]
        for piece in range(PIECES):
            cos_a = turns[lat, piece : piece + 1, at]
            sin_a = turns[lat, 8 + piece : 9 + piece, at]
            row = piece * fields + third * 16
            turned[row : row + 16, at] = (real * cos_a - imag * sin_a).astype(jnp.bfloat16)
            turned[row : row + 16, behind] = (real * sin_a + imag * cos_a).astype(jnp.bfloat16)


def table_copies(source, target, sems):
    rows = target.shape[0] // 3
    return [
        pltpu.make_async_copy(
            source.at[part * rows : part * rows + rows],
            target.at[part * rows : part * rows + rows],
            sems.at[part],
        )
        for part in range(3)
    ]


def own_kernel(
    own, table_ref, turns_ref, turned, table, turns, rows, parts, bands, sems, table_sems
):
    fetch = [
        pltpu.make_async_copy(turns_ref, turns, sems),
        *table_copies(table_ref.at[0], table, table_sems),
    ]
    for copy in fetch:
        copy.start()
    unpack(own, rows, parts, (bands.at[0], bands.at[1]))
    fetch[0].wait()

    @pl.loop(0, turns.shape[2] // 128)
    def _(slot):
        for lat in (0, 1):
            turn(bands.at[lat], turns, lat, slot, turned.at[lat])

    for copy in fetch[1:]:
        copy.wait()


def own_call(own, table, turns, fields):
    return pl.pallas_call(
        own_kernel,
        out_shape=[
            jax.ShapeDtypeStruct((2, PIECES * fields, table.shape[2]), jnp.bfloat16),
            jax.ShapeDtypeStruct(table.shape[1:], jnp.bfloat16),
            jax.ShapeDtypeStruct(turns.shape, jnp.float32),
        ],
        in_specs=[
            pl.BlockSpec(memory_space=pltpu.VMEM),
            pl.BlockSpec(memory_space=pl.ANY),
            pl.BlockSpec(memory_space=pl.ANY),
        ],
        out_specs=[pl.BlockSpec(memory_space=pltpu.VMEM)] * 3,
        scratch_shapes=[
            pltpu.VMEM((2048, 128), jnp.float32),
            pltpu.VMEM((2, 1024, 128), jnp.bfloat16),
            pltpu.VMEM((2, 128, 1024), jnp.float32),
            pltpu.SemaphoreType.DMA,
            pltpu.SemaphoreType.DMA((3,)),
        ],
        compiler_params=pltpu.CompilerParams(vmem_limit_bytes=VMEM),
        cost_estimate=pl.CostEstimate(
            flops=40_000_000, bytes_accessed=6_000_000, transcendentals=0
        ),
        name="own",
    )(own, table, turns)


def fourier_kernel(
    fields,
    own_turned,
    other,
    table_north,
    turns,
    table_ref,
    out_ref,
    table_south,
    rows,
    parts,
    bands,
    turned,
    out,
    sems,
    table_sems,
):
    half_width = out.shape[2]
    slots = turns.shape[2] // 128
    lev = lax.axis_index("lev")
    start = lev * half_width
    fetch = table_copies(table_ref.at[1], table_south, table_sems)
    for copy in fetch:
        copy.start()

    def multiply(lat, number, lines, beside=None):
        table = table_south if lat else table_north
        values = lax.dot_general(
            lines[...], table[0:BLOCK], NT, preferred_element_type=jnp.float32
        )
        tail = lax.dot_general(
            lines[(PIECES - 1) * fields :, :],
            table[BLOCK : BLOCK + 16],
            NT,
            preferred_element_type=jnp.float32,
        )
        if beside is not None:
            beside()
        level = pl.ds(pl.multiple_of((number ^ lev) * fields, 16), fields)
        column = lax.broadcasted_iota(jnp.int32, (1, BLOCK), 1) + start
        limit = turns[lat, 7:8, 0:BLOCK].astype(jnp.int32)
        for piece in range(PIECES):
            out[lat, level, piece * BLOCK : piece * BLOCK + BLOCK] = jnp.where(
                column + piece * BLOCK < limit, values[piece * fields : piece * fields + fields], 0.0
            ).astype(jnp.bfloat16)
        kept = column[:, 0:16] + PIECES * BLOCK < limit[:, 0:16]
        out[lat, level, PIECES * BLOCK :] = jnp.where(kept, tail, 0.0)[
            :, 0 : half_width - PIECES * BLOCK
        ].astype(jnp.bfloat16)
        copy = pltpu.make_async_copy(
            out.at[lat, level], out_ref.at[lat, level], sems.at[2 * lat + number]
        )
        copy.start()
        return copy

    def turn_other(lat):
        for slot in range(slots):
            turn(bands.at[lat], turns, lat, slot, turned.at[lat])

    def open_other():
        unpack(other, rows, parts, (bands.at[0], bands.at[1]))
        turn_other(0)

    copies = [
        multiply(0, 0, own_turned.at[0], open_other),
        multiply(0, 1, turned.at[0], lambda: turn_other(1)),
    ]
    for copy in fetch:
        copy.wait()
    copies += [multiply(1, 0, own_turned.at[1]), multiply(1, 1, turned.at[1])]
    for copy in copies:
        copy.wait()


def fourier_call(own_turned, other, table_north, turns, table, half_width, fields):
    shape = (2, 2 * fields, half_width)
    return pl.pallas_call(
        functools.partial(fourier_kernel, fields),
        out_shape=jax.ShapeDtypeStruct(shape, jnp.bfloat16),
        in_specs=[pl.BlockSpec(memory_space=pltpu.VMEM)] * 4
        + [pl.BlockSpec(memory_space=pl.ANY)],
        out_specs=pl.BlockSpec(memory_space=pl.ANY),
        scratch_shapes=[
            pltpu.VMEM(table_north.shape, jnp.bfloat16),
            pltpu.VMEM((2048, 128), jnp.float32),
            pltpu.VMEM((2, 1024, 128), jnp.bfloat16),
            pltpu.VMEM((2, 128, 1024), jnp.float32),
            pltpu.VMEM(own_turned.shape, jnp.bfloat16),
            pltpu.VMEM(shape, jnp.bfloat16),
            pltpu.SemaphoreType.DMA((4,)),
            pltpu.SemaphoreType.DMA((3,)),
        ],
        compiler_params=pltpu.CompilerParams(vmem_limit_bytes=VMEM),
        name="fourier",
    )(own_turned, other, table_north, turns, table)


def on_device(spectra, legendre, wave_slots, row_length):
    slots = spectra.shape[0]
    fields = spectra.shape[1] // 2
    total = wave_slots.shape[0]
    half_width = (4 * total + 16) // 2
    lev = lax.axis_index("lev").astype(jnp.int32)
    scalars = jnp.concatenate([row_length, lev[None]])
    order = exchange_order()
    waves = wave_slots.reshape(total // slots, slots)[order].T.reshape(1, total)
    sent = legendre_call(wave_slots, legendre, spectra)
    arrived = lax.all_to_all(
        sent,
        "wave",
        split_axis=0,
        concat_axis=0,
        axis_index_groups=[[int(chip) for chip in order]],
        tiled=True,
    )
    table, turns = table_call(scalars, waves, half_width)
    arrived, table, turns = lax.optimization_barrier((arrived, table, turns))
    other = lax.ppermute(arrived, "lev", [(0, 1), (1, 0)])
    own_turned, table_north, turns = own_call(arrived, table, turns, fields)
    return fourier_call(own_turned, other, table_north, turns, table, half_width, fields)


def solution(mesh):
    placed = (P("wave", "lev", None), P("wave", None, None), P(), P("wave"))
    return jax.shard_map(
        on_device, mesh=mesh, in_specs=placed, out_specs=P("wave", None, "lev"), check_vma=False
    )
```
